512 devices in a mesh: loop: 16 (over z_hi, x, core), grp: 32 (over y, z_lo).
Axes of the slice: x: 4, y: 8, z: 8 (z_hi: 2, z_lo: 4; z = z_hi * 4 + z_lo), core: 2. Of those that a mesh axis runs over, the one named last changes fastest.
Arguments:
- points: bfloat16 [64, 98304], P(None, ('loop', 'grp')), may hold values from -2 to 2, as said below
- probes: bfloat16 [16, 98304], P(None, ('loop', 'grp')), may hold values from -6 to 6
Outputs:
- product: float32 [16, 98304], P(None, ('loop', 'grp'))
The draws below stay inside these ranges and needn't reach their ends.
Inputs may be any that keep to these rules, and one draw needn't show every extreme that they name: points drawn around a set of cluster centres with spreads that differ from point to point.
All inputs are finite; a program needn't handle non-finite values.
Results may differ from the reference program's by a relative error of at most 0.0038.
Values may be sent and summed in bfloat16 or wider, within the bound.
A program may use at most 64 MiB of HBM per device.

```python
import math
import jax
import jax.numpy as jnp
from jax import lax

FEAT = 64
PROBES = 16
CLUSTERS = 64
NPTS = 98304


def draw_points(key, part):
    key = jax.random.fold_in(key, 11)
    keys = jax.random.split(key, 4)
    centres = jax.random.normal(keys[0], (FEAT, CLUSTERS), jnp.float32) * 0.15
    labels = jax.random.randint(keys[1], (NPTS,), 0, CLUSTERS)
    spread = jnp.exp(jax.random.uniform(keys[2], (NPTS,), jnp.float32, math.log(0.02), math.log(0.12)))
    noise = jax.random.normal(keys[3], (FEAT, NPTS), jnp.float32)
    noise = jnp.clip(noise, -5.0, 5.0)
    values = centres[:, labels] + spread[None, :] * noise
    return values.astype(jnp.bfloat16)


def level_of(key, extent, cuts, low, largest):
    gain, own = 1.0, jax.random.fold_in(key, 6)
    for dim, blocks in cuts:
        steps = jnp.exp(jax.random.uniform(jax.random.fold_in(own, dim), (blocks,), jnp.float32, low / len(cuts), largest / len(cuts)))
        gain = gain * jnp.repeat(steps, extent[dim] // blocks).reshape([-1 if axis == dim else 1 for axis in range(len(extent))])
    return gain


def scatter_about(stream_key, dims, deviation, reach, cuts=(), dtype=jnp.bfloat16):
    entries = deviation * jax.random.normal(stream_key, dims, jnp.float32)
    if cuts:
        entries = entries * level_of(stream_key, dims, cuts, -0.22, 0.18)
    return jnp.clip(entries, -reach, reach).astype(dtype)


def setup_inputs(seed: int = 0) -> dict:
    seeds = jax.random.split(jax.random.key(seed), 3)
    points = draw_points(jax.random.fold_in(seeds[2], 71), 0)
    probes = scatter_about(seeds[1], (PROBES, NPTS), 1.0, 6.0, ((1, 512),))
    return {"points": points, "probes": probes}


def matern(xa, na, xb, nb):
    cross = lax.dot_general(xa, xb, (((0,), (0,)), ((), ())), preferred_element_type=jnp.float32)
    dist = jnp.maximum(na[:, None] + nb[None, :] - 2.0 * cross, 0.0)
    scaled = jnp.sqrt(5.0 * dist)
    return ((1.0 + scaled + scaled * scaled / 3.0) * jnp.exp(-scaled)).astype(jnp.bfloat16)

def reference(points, probes):
    total = points.shape[1]
    sqnorm = lax.optimization_barrier(jnp.sum(points.astype(jnp.float32) * points.astype(jnp.float32), axis=0))
    width = math.gcd(total, 512)
    count = total // width
    row_x = points.reshape(points.shape[0], count, width).transpose(1, 0, 2)
    row_n = sqnorm.reshape(count, width)

    def one_block(args):
        block_x, block_n = args
        kern = matern(block_x, block_n, points, sqnorm)
        return lax.dot_general(probes, kern, (((1,), (1,)), ((), ())), preferred_element_type=jnp.float32)
    result = lax.map(one_block, (row_x, row_n))
    result = result.transpose(1, 0, 2).reshape(probes.shape[0], total)
    return result * float(total) ** (-0.5)
```

```python
import math

import jax
import jax.numpy as jnp
from jax import lax
from jax.experimental import pallas as pl
from jax.experimental.pallas import tpu as pltpu
from jax.sharding import PartitionSpec as P

MESH = pl.DeviceIdType.MESH
FEAT, PROBES, OWN = 64, 16, 192
AUX = 16
DEPTH = 128
ROWS = FEAT + AUX + PROBES
PLACES = 32
QUAD = 4 * OWN
PAIR = 2 * OWN
FULL = ((0, 1), (1, 0), (1, 1), (1, 3), (1, 2), (2, 1))
SELF = ((0, 0), (2, 0), (0, 2), (2, 2))
STEPS = FULL + SELF
HOME = len(FULL)
BF = jnp.bfloat16
F32 = jnp.float32


def device(yh, zq, place):
    x, yl, zl, core = place // 8, (place // 4) % 2, (place // 2) % 2, place % 2
    return ((zq // 2) * 8 + x * 2 + core, (yh * 2 + yl) * 4 + (zq % 2) * 2 + zl)


def step_of(slot):
    k = jnp.where(slot >= 18, slot, slot - 3)
    k = jnp.where(slot == 0, 0, k)
    k = jnp.where(slot == 1, 16, k)
    k = jnp.where(slot == 2, 15, k)
    return jnp.where(slot == 3, 17, k)


def entries(m):
    d = jnp.maximum(m, 1e-30)
    t = d * lax.rsqrt(d)
    e = jnp.exp2(t * (-math.sqrt(5.0) * math.log2(math.e)))
    p = (t * (5.0 / 3.0) + math.sqrt(5.0)) * t + 1.0
    return (p * e).astype(BF)


def kernel(scale, pts, prb, out, own, rbuf, cbuf, cpm, cv, rw, rv, yc, yrs, yrr, ycs, ycr,
           rsend, rrecv, csend, crecv, ysend, yrecv, zsend, zrecv):
    loop, grp = lax.axis_index("loop"), lax.axis_index("grp")
    core, x, zhi = loop % 2, (loop // 2) % 4, loop // 8
    y, zlo = grp // 4, grp % 4
    zq, zl, yh, yl = zhi * 2 + zlo // 2, zlo % 2, y // 2, y % 2
    q = ((x * 2 + yl) * 2 + zl) * 2 + core

    barrier = pltpu.get_barrier_semaphore()

    @pl.loop(1, PLACES)
    def _(k):
        pl.semaphore_signal(barrier, inc=1, device_id=device(yh, zq, (q + k) % PLACES), device_id_type=MESH)

    @pl.loop(1, 16)
    def _(k):
        pl.semaphore_signal(barrier, inc=1, device_id=device((yh + k // 4) % 4, (zq + k % 4) % 4, q), device_id_type=MESH)

    own[0:FEAT, :] = pts[...]
    own[FEAT + AUX:ROWS, :] = prb[...]
    wide = pts[...].astype(F32)
    n = jnp.sum(wide * wide, axis=0, keepdims=True)
    hi = n.astype(BF).astype(F32)
    mid = (n - hi).astype(BF).astype(F32)
    lo = n - hi - mid
    row = lax.broadcasted_iota(jnp.int32, (AUX, OWN), 0)
    aux = jnp.where(row == 0, hi, jnp.where(row == 1, mid, jnp.where(row == 2, lo, jnp.where(row < 6, 1.0, 0.0))))
    own[FEAT:FEAT + AUX, :] = aux.astype(BF)
    rbuf[0] = own[...]
    cbuf[HOME] = own[...]
    rw[FEAT + AUX:DEPTH, :] = jnp.zeros((DEPTH - FEAT - AUX, QUAD), BF)
    yc[...] = jnp.zeros_like(yc)

    pl.semaphore_wait(barrier, PLACES - 1 + 15)

    def column_copy(j):
        dy, dz = STEPS[j]
        return pltpu.make_async_remote_copy(
            src_ref=own, dst_ref=cbuf.at[j], send_sem=csend.at[j], recv_sem=crecv.at[j],
            device_id=device((yh - dy + 4) % 4, (zq - dz + 4) % 4, q), device_id_type=MESH)

    def row_copy(s):
        return pltpu.make_async_remote_copy(
            src_ref=own, dst_ref=rbuf.at[s], send_sem=rsend.at[s], recv_sem=rrecv.at[s],
            device_id=device(yh, zq, (q - step_of(s) + PLACES) % PLACES), device_id_type=MESH)

    def row_sum(s):
        return pltpu.make_async_remote_copy(
            src_ref=yrs.at[s], dst_ref=yrr.at[s], send_sem=ysend.at[s], recv_sem=yrecv.at[s],
            device_id=device(yh, zq, (q + step_of(s)) % PLACES), device_id_type=MESH)

    def column_sum(j):
        dy, dz = STEPS[j]
        return pltpu.make_async_remote_copy(
            src_ref=ycs.at[j], dst_ref=ycr.at[j], send_sem=zsend.at[j], recv_sem=zrecv.at[j],
            device_id=device((yh + dy) % 4, (zq + dz) % 4, q), device_id_type=MESH)

    far = [j for j in range(len(STEPS)) if j != HOME]
    for j in far:
        column_copy(j).start()

    @pl.loop(1, PLACES)
    def _(s):
        row_copy(s).start()

    for j in far:
        column_copy(j).wait_recv()

    @pl.loop(0, len(STEPS) // 2)
    def _(h):
        both = jnp.concatenate([cbuf[2 * h].astype(F32), cbuf[2 * h + 1].astype(F32)], axis=1)
        aux = both[FEAT:FEAT + AUX]
        row = lax.broadcasted_iota(jnp.int32, (AUX, PAIR), 0)
        swapped = jnp.where(row < 3, 1.0, jnp.where(row < 6, pltpu.roll(aux, 3, 0), 0.0))
        tall = jnp.concatenate([both[:FEAT] * -2.0, swapped, jnp.zeros((DEPTH - FEAT - AUX, PAIR), F32)], axis=0)
        cpm[pl.ds(pl.multiple_of(h * PAIR, PAIR), PAIR), :] = tall.T.astype(BF)
        cv[h] = both[FEAT + AUX:].astype(BF)

    @pl.loop(0, PLACES // 4)
    def _(quad):
        first = quad * 4

        @pl.when(quad > 0)
        def _():
            row_copy(first).wait_recv()

        for t in range(1, 4):
            row_copy(first + t).wait_recv()
        four = jnp.concatenate([rbuf[first + t].astype(F32) for t in range(4)], axis=1)
        rw[0:FEAT + AUX, :] = four[:FEAT + AUX].astype(BF)
        rv[...] = four[FEAT + AUX:].astype(BF)
        lane = lax.broadcasted_iota(jnp.int32, (PROBES, QUAD), 1)

        def visit(h, acc):
            mine = h >= len(FULL) // 2
            left = jnp.where(jnp.logical_and(mine, quad == 0), 0.5, 1.0)
            right = jnp.where(mine, jnp.where(quad == 0, 0.5, jnp.where(quad == 4, 0.0, 1.0)), 1.0)
            weight = jnp.where(lane < PAIR, left, right)
            vr = (rv[...].astype(F32) * weight).astype(BF)
            cols = cpm[pl.ds(pl.multiple_of(h * PAIR, PAIR), PAIR), :]
            vc = cv[h]
            ysum = yc[h]
            parts = []
            for b in range(3):
                at = slice(b * 256, b * 256 + 256)
                k = entries(jnp.dot(cols, rw[:, at], preferred_element_type=F32))
                parts.append(jnp.dot(vc, k, preferred_element_type=F32))
                ysum = ysum + lax.dot_general(vr[:, at], k, (((1,), (1,)), ((), ())), preferred_element_type=F32)
            yc[h] = ysum
            return acc + jnp.concatenate(parts, axis=1) * weight

        count = jnp.where(quad < 5, len(STEPS) // 2, len(FULL) // 2)
        acc = lax.fori_loop(0, count, visit, jnp.zeros((PROBES, QUAD), F32))
        for t in range(4):
            yrs[first + t] = acc[:, t * OWN:(t + 1) * OWN]

        @pl.when(quad > 0)
        def _():
            row_sum(first).start()

        for t in range(1, 4):
            row_sum(first + t).start()

    for h in range(len(STEPS) // 2):
        ycs[2 * h] = yc[h, :, 0:OWN]
        ycs[2 * h + 1] = yc[h, :, OWN:PAIR]
    for j in far:
        column_sum(j).start()

    total = yrs[0] + ycs[HOME]

    def add_row(s, total):
        row_sum(s).wait_recv()
        return total + yrr[s]

    total = lax.fori_loop(1, PLACES, add_row, total)
    for j in far:
        column_sum(j).wait_recv()
        total = total + ycr[j]
    out[...] = total * scale

    for j in far:
        column_copy(j).wait_send()
        column_sum(j).wait_send()

    @pl.loop(1, PLACES)
    def _(s):
        row_copy(s).wait_send()
        row_sum(s).wait_send()


def on_device(points, probes):
    total = points.shape[1] * lax.axis_size("loop") * lax.axis_size("grp")
    steps = len(STEPS)
    vmem, dma = pltpu.VMEM, pltpu.SemaphoreType.DMA
    return pl.pallas_call(
        lambda *refs: kernel(float(total) ** (-0.5), *refs),
        out_shape=jax.ShapeDtypeStruct((PROBES, OWN), F32),
        in_specs=[pl.BlockSpec(memory_space=vmem)] * 2,
        out_specs=pl.BlockSpec(memory_space=vmem),
        scratch_shapes=[
            vmem((ROWS, OWN), BF),
            vmem((PLACES, ROWS, OWN), BF),
            vmem((steps, ROWS, OWN), BF),
            vmem((steps * OWN, DEPTH), BF),
            vmem((steps // 2, PROBES, PAIR), BF),
            vmem((DEPTH, QUAD), BF),
            vmem((PROBES, QUAD), BF),
            vmem((steps // 2, PROBES, PAIR), F32),
            vmem((PLACES, PROBES, OWN), F32),
            vmem((PLACES, PROBES, OWN), F32),
            vmem((steps, PROBES, OWN), F32),
            vmem((steps, PROBES, OWN), F32),
            dma((PLACES,)), dma((PLACES,)), dma((steps,)), dma((steps,)),
            dma((PLACES,)), dma((PLACES,)), dma((steps,)), dma((steps,)),
        ],
        compiler_params=pltpu.CompilerParams(
            collective_id=0, has_side_effects=True, vmem_limit_bytes=40 * 1024 * 1024
        ),
        name="matern_product",
    )(points, probes)


def solution(mesh):
    specs = P(None, ("loop", "grp"))
    return jax.shard_map(on_device, mesh=mesh, in_specs=(specs, specs), out_specs=specs, check_vma=False)
```

```python
import math

import jax
import jax.numpy as jnp
from jax import lax
from jax.experimental import pallas as pl
from jax.experimental.pallas import tpu as pltpu
from jax.sharding import PartitionSpec as P

MESH = pl.DeviceIdType.MESH
BF = jnp.bfloat16
F32 = jnp.float32
FEAT, PROBES, OWN = 64, 16, 192
AUX = 16
ROWS = FEAT + AUX + PROBES
FOLD = ROWS + ROWS // 2
DEPTH = 3 * FEAT + AUX
PLACES = 16
CHIP = 2 * OWN
LANES = 256
BLOCKS = PLACES * CHIP // LANES
STEPS = (((0, 1), (1, 7), (0, 6), (0, 0), (1, 4)),
         ((1, 2), (0, 3), (1, 5), (1, 0), (0, 4)))
FULL, COLS = 3, 5
BOTH = 14
WORK = BOTH + (BLOCKS - BOTH) * FULL // COLS


def device(xh, z, place, core):
    return ((z // 4 * 4 + xh * 2 + place % 2) * 2 + core, place // 2 * 4 + z % 4)


def tile_of(step, b):
    flat = jnp.maximum(step - BOTH, 0) * COLS + b
    late = step >= BOTH
    return jnp.where(late, flat % FULL, b), jnp.where(late, BOTH + flat // FULL, step)


def weights(h, lb):
    mine = h >= FULL
    half = jnp.logical_or(lb < 2, jnp.logical_or(lb == 12, lb == 13))
    left = jnp.where(jnp.logical_and(mine, half), 0.5, 1.0)
    right = jnp.where(jnp.logical_and(mine, jnp.logical_or(lb == 0, lb == 12)), 0.5, 1.0)
    right = jnp.where(jnp.logical_and(mine, lb == 13), 0.0, right)
    return left, right


def among(value, options):
    hit = value == options[0]
    for option in options[1:]:
        hit = jnp.logical_or(hit, value == option)
    return hit


def tiles_of(halves):
    first, second = halves[0].astype(F32), halves[1].astype(F32)
    low = lax.broadcasted_iota(jnp.int32, (ROWS // 2, 128), 1) < 64
    f0, f1 = first[ROWS:], second[ROWS:]
    top = jnp.where(low, f0, pltpu.roll(f1, 64, 1))
    bottom = jnp.where(low, pltpu.roll(f0, 64, 1), f1)
    return first[:ROWS], jnp.concatenate([top, bottom], axis=0), second[:ROWS]


def kernel(scale, pts, prb, out, own, rbuf, cbuf, cpm, cv, rw, rv, yr, yc, ybuf, zbuf, m, k,
           rsend, rrecv, fsend, frecv, csend, crecv, ysend, yrecv, zsend, zrecv):
    loop, grp = lax.axis_index("loop"), lax.axis_index("grp")
    core, x, z = loop % 2, (loop // 2) % 4, loop // 8 * 4 + grp % 4
    other = 1 - core
    xh, place = x // 2, grp // 4 * 2 + x % 2
    sibling = device(xh, z, place, other)

    def chosen(h):
        (ax, az), (bx, bz) = STEPS[0][h], STEPS[1][h]
        return jnp.where(core == 0, ax, bx), jnp.where(core == 0, az, bz)

    barrier = pltpu.get_barrier_semaphore()
    pl.semaphore_signal(barrier, inc=1, device_id=sibling, device_id_type=MESH)

    @pl.loop(1, 16)
    def _(step):
        for c in range(2):
            pl.semaphore_signal(barrier, inc=1, device_id=device(xh, z, (place + step) % PLACES, c), device_id_type=MESH)
            pl.semaphore_signal(barrier, inc=1, device_id=device((xh + step // 8) % 2, (z + step) % 8, place, c), device_id_type=MESH)

    wide = pts[...].astype(F32)
    n = jnp.sum(wide * wide, axis=0, keepdims=True) * (5.0 / 3.0)
    hi = n.astype(BF).astype(F32)
    mid = (n - hi).astype(BF).astype(F32)
    lo = n - hi - mid
    row = lax.broadcasted_iota(jnp.int32, (AUX, OWN), 0)
    aux = jnp.where(row == 0, hi, jnp.where(row == 1, mid, jnp.where(row == 2, lo, jnp.where(row < 6, 1.0, 0.0))))
    chunk = jnp.concatenate([wide, aux, prb[...].astype(F32)], axis=0)
    own[0:ROWS, :] = chunk[:, :128].astype(BF)
    tail = chunk[:, 128:]
    own[ROWS:FOLD, :] = jnp.concatenate([tail[:ROWS // 2], tail[ROWS // 2:]], axis=1).astype(BF)
    rbuf[0, core] = own[...]
    yr[...] = jnp.zeros_like(yr)
    yc[...] = jnp.zeros_like(yc)
    k[...] = jnp.zeros_like(k)

    pl.semaphore_wait(barrier, 1 + 15 * 4)

    def share():
        return pltpu.make_async_remote_copy(
            src_ref=own, dst_ref=rbuf.at[0, core], send_sem=rsend.at[0], recv_sem=rrecv.at[0, core],
            device_id=sibling, device_id_type=MESH)

    def row_copy(slot, half):
        return pltpu.make_async_remote_copy(
            src_ref=own, dst_ref=rbuf.at[slot, half], send_sem=rsend.at[slot], recv_sem=rrecv.at[slot, half],
            device_id=device(xh, z, (place - slot + PLACES) % PLACES, slot % 2), device_id_type=MESH)

    def forward(slot):
        return pltpu.make_async_remote_copy(
            src_ref=rbuf.at[slot], dst_ref=rbuf.at[slot], send_sem=fsend.at[slot], recv_sem=frecv.at[slot],
            device_id=sibling, device_id_type=MESH)

    def column_copy(taker, h, half):
        dx, dz = STEPS[taker][h]
        return pltpu.make_async_remote_copy(
            src_ref=own, dst_ref=cbuf.at[h, half], send_sem=csend.at[taker, h], recv_sem=crecv.at[h, half],
            device_id=device((xh - dx + 2) % 2, (z - dz + 8) % 8, place, taker), device_id_type=MESH)

    def row_sum(slot, c):
        return pltpu.make_async_remote_copy(
            src_ref=yr.at[pl.ds(slot * 3 + c, 2)], dst_ref=ybuf.at[core, slot],
            send_sem=ysend.at[slot, c], recv_sem=yrecv.at[core, slot],
            device_id=device(xh, z, (place + slot) % PLACES, c), device_id_type=MESH)

    def column_sum(h, c):
        dx, dz = chosen(h)
        return pltpu.make_async_remote_copy(
            src_ref=yc.at[h, pl.ds(c, 2)], dst_ref=zbuf.at[core, h],
            send_sem=zsend.at[h, c], recv_sem=zrecv.at[core, h],
            device_id=device((xh + dx) % 2, (z + dz) % 8, place, c), device_id_type=MESH)

    def arrived(dst, sem):
        pltpu.make_async_remote_copy(
            src_ref=dst, dst_ref=dst, send_sem=fsend.at[0], recv_sem=sem, device_id=sibling, device_id_type=MESH).wait_recv()

    away = [(taker, h) for h in range(COLS) for taker in range(2) if STEPS[taker][h] != (0, 0)]
    share().start()
    row_copy(1, core).start()
    for taker, h in away:
        column_copy(taker, h, core).start()

    @pl.loop(2, PLACES)
    def _(slot):
        row_copy(slot, core).start()

    def hand_over(pair):
        slot = pair * 2 + core
        for half in range(2):
            arrived(rbuf.at[slot, half], rrecv.at[slot, half])
        forward(slot).start()

    def prepare(pair):
        six = tiles_of(rbuf[2 * pair]) + tiles_of(rbuf[2 * pair + 1])
        for b in range(3):
            block = jnp.concatenate([six[2 * b], six[2 * b + 1]], axis=1)
            lb = 3 * pair + b
            feat = block[:FEAT].astype(BF)
            for piece in range(3):
                rw[lb, piece * FEAT:(piece + 1) * FEAT, :] = feat
            rw[lb, 3 * FEAT:, :] = block[FEAT:FEAT + AUX].astype(BF)
            probes = block[FEAT + AUX:]
            left, right = weights(FULL, lb)
            lane = lax.broadcasted_iota(jnp.int32, (PROBES, LANES), 1)
            rv[0, lb] = probes.astype(BF)
            rv[1, lb] = (probes * jnp.where(lane < 128, left, right)).astype(BF)

    arrived(rbuf.at[0, other], rrecv.at[0, other])

    @pl.when(core == 0)
    def _():
        cbuf[FULL] = rbuf[0]

    @pl.when(core == 1)
    def _():
        hand_over(0)

    def column(h, _):
        @pl.when(jnp.logical_or(h != FULL, core == 1))
        def _():
            for half in range(2):
                arrived(cbuf.at[h, half], crecv.at[h, half])
        both = jnp.concatenate(tiles_of(cbuf[h]), axis=1)
        scaled = both[:FEAT] * (-10.0 / 3.0)
        hi = scaled.astype(BF).astype(F32)
        mid = (scaled - hi).astype(BF).astype(F32)
        aux = both[FEAT:FEAT + AUX]
        row = lax.broadcasted_iota(jnp.int32, (AUX, CHIP), 0)
        swapped = jnp.where(row < 3, 1.0, jnp.where(row < 6, pltpu.roll(aux, 3, 0), 0.0))
        cpm[h] = jnp.concatenate([hi, mid, scaled - hi - mid, swapped], axis=0).T.astype(BF)
        cv[h] = both[FEAT + AUX:].astype(BF)
        return 0

    lax.fori_loop(0, COLS, column, 0)

    def cross(step, b):
        h, lb = tile_of(step, b)
        m[b] = jnp.maximum(jnp.dot(cpm[h], rw[lb], preferred_element_type=F32), 1e-30)

    def entries(b):
        d = m[b]
        t = d * lax.rsqrt(d)
        e = jnp.exp2(t * (-math.sqrt(3.0) * math.log2(math.e)))
        p = t + math.sqrt(0.75)
        return ((p * p + 0.25) * e).astype(BF)

    def products(step, b, kern):
        h, lb = tile_of(step, b)
        mine = jnp.where(h >= FULL, 1, 0)
        left, right = weights(h, lb)
        part = jnp.dot(cv[h], kern, preferred_element_type=F32)
        yr[2 * lb] += part[:, :128] * left
        yr[2 * lb + 1] += part[:, 128:] * right
        part = lax.dot_general(rv[mine, lb], kern, (((1,), (1,)), ((), ())), preferred_element_type=F32)
        for tile in range(3):
            yc[h, tile] += part[:, tile * 128:(tile + 1) * 128]

    def send_rows(pair):
        for slot in (2 * pair, 2 * pair + 1):
            @pl.when(slot > 0)
            def _():
                row_sum(slot, 0).start()
                row_sum(slot, 1).start()

            @pl.when(slot == 0)
            def _():
                row_sum(slot, other).start()

    def ready(pair):
        @pl.when(pair < PLACES // 2 - 1)
        def _():
            hand_over(pair + 1)

        slot = pair * 2 + other

        @pl.when(slot > 0)
        def _():
            arrived(rbuf.at[slot], frecv.at[slot])
        prepare(pair)

    ready(0)
    for b in range(COLS):
        cross(0, b)

    def work(step, _):
        late = step + 1 >= BOTH
        starts = jnp.where(late, (step + 1 - BOTH) % 2 == 0, (step + 1) % 3 == 0)

        @pl.when(jnp.logical_and(starts, step + 1 < WORK))
        def _():
            ready(jnp.where(late, 5 + (step + 1 - BOTH) // 2, (step + 1) // 3))

        before, after = jnp.maximum(step - 1, 0), jnp.minimum(step + 1, WORK - 1)
        for b in range(COLS):
            kern = entries(b)
            cross(after, b)
            products(before, b, k[b])
            k[b] = kern

        @pl.when(among(step, (3, 6, 9, 12, 15, 17, 19)))
        def _():
            send_rows(jnp.where(step <= 15, step // 3 - 1, (step - 7) // 2))
        return 0

    lax.fori_loop(0, WORK, work, 0)
    for b in range(COLS):
        products(WORK - 1, b, k[b])
    send_rows(PLACES // 2 - 1)

    for h in range(COLS):
        for c in range(2):
            if STEPS[0][h] == (0, 0):
                @pl.when(jnp.logical_or(core == 1, c == 1))
                def _():
                    column_sum(h, c).start()
            else:
                column_sum(h, c).start()

    total = yr[pl.ds(core, 2)]

    def add_rows(slot, total):
        for c in range(2):
            arrived(ybuf.at[c, slot], yrecv.at[c, slot])
        return total + ybuf[0, slot] + ybuf[1, slot]

    arrived(ybuf.at[other, 0], yrecv.at[other, 0])
    total = total + ybuf[other, 0]
    total = lax.fori_loop(1, PLACES, add_rows, total)
    for taker, h in away:
        arrived(zbuf.at[taker, h], zrecv.at[taker, h])
        total = total + zbuf[taker, h]

    @pl.when(core == 1)
    def _():
        arrived(zbuf.at[0, FULL], zrecv.at[0, FULL])

    @pl.when(core == 0)
    def _():
        zbuf[0, FULL] = yc[FULL, 0:2]

    total = (total + zbuf[0, FULL]) * scale
    main = jnp.where(core == 0, total[0], total[1])
    tail = jnp.where(core == 0, total[1], pltpu.roll(total[0], 64, 1))
    out[:, 0:128] = main
    out[:, 128:OWN] = tail[:, 0:64]

    share().wait_send()
    for taker, h in away:
        column_copy(taker, h, core).wait_send()

    @pl.loop(1, PLACES)
    def _(slot):
        row_copy(slot, core).wait_send()
        row_sum(slot, 0).wait_send()
        row_sum(slot, 1).wait_send()

    row_sum(0, other).wait_send()

    @pl.loop(0, PLACES // 2)
    def _(pair):
        slot = pair * 2 + core

        @pl.when(slot > 0)
        def _():
            forward(slot).wait_send()

    for h in range(COLS):
        for c in range(2):
            if STEPS[0][h] == (0, 0):
                @pl.when(jnp.logical_or(core == 1, c == 1))
                def _():
                    column_sum(h, c).wait_send()
            else:
                column_sum(h, c).wait_send()


def on_device(points, probes):
    total = points.shape[1] * lax.axis_size("loop") * lax.axis_size("grp")
    vmem, dma = pltpu.VMEM, pltpu.SemaphoreType.DMA
    return pl.pallas_call(
        lambda *refs: kernel(float(total) ** (-0.5), *refs),
        out_shape=jax.ShapeDtypeStruct((PROBES, OWN), F32),
        in_specs=[pl.BlockSpec(memory_space=vmem)] * 2,
        out_specs=pl.BlockSpec(memory_space=vmem),
        scratch_shapes=[
            vmem((FOLD, 128), BF),
            vmem((PLACES, 2, FOLD, 128), BF),
            vmem((COLS, 2, FOLD, 128), BF),
            vmem((COLS, CHIP, DEPTH), BF),
            vmem((COLS, PROBES, CHIP), BF),
            vmem((BLOCKS, DEPTH, LANES), BF),
            vmem((2, BLOCKS, PROBES, LANES), BF),
            vmem((PLACES * 3, PROBES, 128), F32),
            vmem((COLS, 3, PROBES, 128), F32),
            vmem((2, PLACES, 2, PROBES, 128), F32),
            vmem((2, COLS, 2, PROBES, 128), F32),
            vmem((COLS, CHIP, LANES), F32),
            vmem((COLS, CHIP, LANES), BF),
            dma((PLACES,)), dma((PLACES, 2)), dma((PLACES,)), dma((PLACES,)), dma((2, COLS)), dma((COLS, 2)),
            dma((PLACES, 2)), dma((2, PLACES)), dma((COLS, 2)), dma((2, COLS)),
        ],
        compiler_params=pltpu.CompilerParams(
            collective_id=0, has_side_effects=True, vmem_limit_bytes=40 * 1024 * 1024
        ),
        name="matern_product",
    )(points, probes)


def solution(mesh):
    specs = P(None, ("loop", "grp"))
    return jax.shard_map(on_device, mesh=mesh, in_specs=(specs, specs), out_specs=specs, check_vma=False)
```

```python
import math

import jax
import jax.numpy as jnp
from jax import lax
from jax.experimental import pallas as pl
from jax.experimental.pallas import tpu as pltpu
from jax.sharding import PartitionSpec as P

MESH = pl.DeviceIdType.MESH
BF = jnp.bfloat16
F32 = jnp.float32
FEAT, PROBES, OWN = 64, 16, 192
AUX = 16
ROWS = FEAT + AUX + PROBES
FOLD = ROWS + ROWS // 2
DEPTH = 3 * FEAT + AUX
PLACES = 16
CHIP = 2 * OWN
LANES = 256
BLOCKS = PLACES * CHIP // LANES
STEPS = (((0, 1), (0, 6), (1, 7), (0, 0), (1, 4)),
         ((0, 3), (1, 2), (1, 5), (1, 0), (0, 4)))
FULL, COLS = 3, 5
DIRECT = ((1, 3), (0, 0), (1, 0), (0, 1))
RELAYED = ((1, 1), (0, 2), (1, 2))
BOTH = 14
WORK = (BOTH * COLS + (BLOCKS - BOTH) * FULL) // COLS


def device(xh, z, place, core):
    return ((z // 4 * 4 + xh * 2 + place % 2) * 2 + core, place // 2 * 4 + z % 4)


def tile_of(step, b):
    flat = step * COLS + b
    second, third, rest = flat - 2 * BOTH, flat - 4 * BOTH, flat - 5 * BOTH
    h = jnp.where(second < 0, flat % 2 * 3, jnp.where(third < 0, second % 2 + 1, jnp.where(rest < 0, 4, rest % 3)))
    lb = jnp.where(second < 0, flat // 2, jnp.where(third < 0, second // 2, jnp.where(rest < 0, third, BOTH + rest // 3)))
    return h, lb


def weights(h, lb):
    mine = h >= FULL
    half = jnp.logical_or(lb < 2, jnp.logical_or(lb == 12, lb == 13))
    left = jnp.where(jnp.logical_and(mine, half), 0.5, 1.0)
    right = jnp.where(jnp.logical_and(mine, jnp.logical_or(lb == 0, lb == 12)), 0.5, 1.0)
    right = jnp.where(jnp.logical_and(mine, lb == 13), 0.0, right)
    return left, right


def among(value, options):
    hit = value == options[0]
    for option in options[1:]:
        hit = jnp.logical_or(hit, value == option)
    return hit


def tiles_of(halves):
    first, second = halves[0].astype(F32), halves[1].astype(F32)
    low = lax.broadcasted_iota(jnp.int32, (ROWS // 2, 128), 1) < 64
    f0, f1 = first[ROWS:], second[ROWS:]
    top = jnp.where(low, f0, pltpu.roll(f1, 64, 1))
    bottom = jnp.where(low, pltpu.roll(f0, 64, 1), f1)
    return first[:ROWS], jnp.concatenate([top, bottom], axis=0), second[:ROWS]


def kernel(scale, pts, prb, out, own, rbuf, cbuf, cpm, cv, rw, rv, yr, yc, pbuf, ybuf, zbuf, m, k,
           hsend, hrecv, rsend, rrecv, xsend, xrecv, fsend, frecv, csend, crecv, lsend, lrecv, psend, precv, ysend, yrecv,
           zsend, zrecv):
    loop, grp = lax.axis_index("loop"), lax.axis_index("grp")
    core, x, z = loop % 2, (loop // 2) % 4, loop // 8 * 4 + grp % 4
    other = 1 - core
    xh, xl, place = x // 2, x % 2, grp // 4 * 2 + x % 2
    sibling = device(xh, z, place, other)

    def chosen(h):
        (ax, az), (bx, bz) = STEPS[0][h], STEPS[1][h]
        return jnp.where(core == 0, ax, bx), jnp.where(core == 0, az, bz)

    barrier = pltpu.get_barrier_semaphore()
    pl.semaphore_signal(barrier, inc=1, device_id=sibling, device_id_type=MESH)

    @pl.loop(1, 16)
    def _(step):
        for c in range(2):
            pl.semaphore_signal(barrier, inc=1, device_id=device(xh, z, (place + step) % PLACES, c), device_id_type=MESH)
            pl.semaphore_signal(barrier, inc=1, device_id=device((xh + step // 8) % 2, (z + step) % 8, place, c), device_id_type=MESH)

    wide = pts[...].astype(F32)
    n = jnp.sum(wide * wide, axis=0, keepdims=True) * (5.0 / 3.0)
    hi = n.astype(BF).astype(F32)
    mid = (n - hi).astype(BF).astype(F32)
    lo = n - hi - mid
    row = lax.broadcasted_iota(jnp.int32, (AUX, OWN), 0)
    aux = jnp.where(row == 0, hi, jnp.where(row == 1, mid, jnp.where(row == 2, lo, jnp.where(row < 6, 1.0, 0.0))))
    chunk = jnp.concatenate([wide, aux, prb[...].astype(F32)], axis=0)
    own[0:ROWS, :] = chunk[:, :128].astype(BF)
    tail = chunk[:, 128:]
    own[ROWS:FOLD, :] = jnp.concatenate([tail[:ROWS // 2], tail[ROWS // 2:]], axis=1).astype(BF)
    rbuf[0, core] = own[...]
    yr[...] = jnp.zeros_like(yr)
    yc[...] = jnp.zeros_like(yc)
    k[...] = jnp.zeros_like(k)

    pl.semaphore_wait(barrier, 1 + 15 * 4)

    def share():
        return pltpu.make_async_remote_copy(
            src_ref=own, dst_ref=rbuf.at[0, core], send_sem=hsend, recv_sem=hrecv,
            device_id=sibling, device_id_type=MESH)

    def row_copy(j):
        return pltpu.make_async_remote_copy(
            src_ref=own, dst_ref=rbuf.at[2 * j, core], send_sem=rsend.at[j], recv_sem=rrecv.at[j, core],
            device_id=device(xh, z, (place - 2 * j + PLACES) % PLACES, j % 2), device_id_type=MESH)

    def across(j):
        slot = jnp.where(xl == 1, 2 * j + 1, (2 * j + 15) % PLACES)
        return pltpu.make_async_remote_copy(
            src_ref=rbuf.at[2 * j], dst_ref=rbuf.at[slot], send_sem=xsend.at[j], recv_sem=xrecv.at[slot],
            device_id=device(xh, z, place + 1 - 2 * xl, core), device_id_type=MESH)

    def forward(slot):
        return pltpu.make_async_remote_copy(
            src_ref=rbuf.at[slot], dst_ref=rbuf.at[slot], send_sem=fsend.at[slot], recv_sem=frecv.at[slot],
            device_id=sibling, device_id_type=MESH)

    def column_copy(taker, h):
        dx, dz = STEPS[taker][h]
        return pltpu.make_async_remote_copy(
            src_ref=own, dst_ref=cbuf.at[h, core], send_sem=csend.at[taker, h], recv_sem=crecv.at[h, core],
            device_id=device((xh - dx + 2) % 2, (z - dz + 8) % 8, place, taker), device_id_type=MESH)

    def relay(taker, h):
        return pltpu.make_async_remote_copy(
            src_ref=cbuf.at[3], dst_ref=cbuf.at[h], send_sem=csend.at[taker, h], recv_sem=lrecv.at[h],
            device_id=device(xh, (z - STEPS[taker][h][1] + 8) % 8, place, taker), device_id_type=MESH)

    def last_relay():
        return pltpu.make_async_remote_copy(
            src_ref=cbuf.at[1], dst_ref=cbuf.at[4], send_sem=lsend, recv_sem=lrecv.at[4],
            device_id=device(xh, (z + jnp.where(core == 0, 2, 6)) % 8, place, other), device_id_type=MESH)

    def trade(pair):
        return pltpu.make_async_remote_copy(
            src_ref=yr.at[pl.ds((2 * pair + other) * 3, 3)], dst_ref=pbuf.at[pair], send_sem=psend.at[pair], recv_sem=precv.at[pair],
            device_id=sibling, device_id_type=MESH)

    def row_sum(slot, c):
        return pltpu.make_async_remote_copy(
            src_ref=yr.at[pl.ds(slot * 3 + c, 2)], dst_ref=ybuf.at[slot],
            send_sem=ysend.at[slot, c], recv_sem=yrecv.at[slot],
            device_id=device(xh, z, (place + slot) % PLACES, c), device_id_type=MESH)

    def column_sum(h, c):
        dx, dz = chosen(h)
        return pltpu.make_async_remote_copy(
            src_ref=yc.at[h, pl.ds(c, 2)], dst_ref=zbuf.at[core, h],
            send_sem=zsend.at[h, c], recv_sem=zrecv.at[core, h],
            device_id=device((xh + dx) % 2, (z + dz) % 8, place, c), device_id_type=MESH)

    def arrived(dst, sem):
        pltpu.make_async_remote_copy(
            src_ref=dst, dst_ref=dst, send_sem=fsend.at[0], recv_sem=sem, device_id=sibling, device_id_type=MESH).wait_recv()

    column_copy(*DIRECT[0]).start()
    share().start()
    for j in (1, 7):
        row_copy(j).start()
    for taker, h in DIRECT[1:]:
        column_copy(taker, h).start()
    for j in (2, 6, 3, 5, 4):
        row_copy(j).start()

    def pass_even(j):
        @pl.when(core == j % 2)
        def _():
            for half in range(2):
                arrived(rbuf.at[2 * j, half], rrecv.at[j, half])
            forward(2 * j).start()
            across(j).start()

    def pass_odd(j):
        @pl.when(core == (j + xl) % 2)
        def _():
            arrived(rbuf.at[2 * j + 1], xrecv.at[2 * j + 1])
            forward(2 * j + 1).start()

    def collect(pair):
        @pl.when(jnp.logical_and(pair > 0, core != pair % 2))
        def _():
            arrived(rbuf.at[2 * pair], frecv.at[2 * pair])

        @pl.when(core != (pair + xl) % 2)
        def _():
            arrived(rbuf.at[2 * pair + 1], frecv.at[2 * pair + 1])
        prepare(pair)

    def prepare(pair):
        six = tiles_of(rbuf[2 * pair]) + tiles_of(rbuf[2 * pair + 1])
        for b in range(3):
            block = jnp.concatenate([six[2 * b], six[2 * b + 1]], axis=1)
            lb = 3 * pair + b
            feat = block[:FEAT].astype(BF)
            for piece in range(3):
                rw[lb, piece * FEAT:(piece + 1) * FEAT, :] = feat
            rw[lb, 3 * FEAT:, :] = block[FEAT:FEAT + AUX].astype(BF)
            probes = block[FEAT + AUX:]
            left, right = weights(FULL, lb)
            lane = lax.broadcasted_iota(jnp.int32, (PROBES, LANES), 1)
            rv[0, lb] = probes.astype(BF)
            rv[1, lb] = (probes * jnp.where(lane < 128, left, right)).astype(BF)

    def column(h):
        both = jnp.concatenate(tiles_of(cbuf[h]), axis=1)
        scaled = both[:FEAT] * (-10.0 / 3.0)
        hi = scaled.astype(BF).astype(F32)
        mid = (scaled - hi).astype(BF).astype(F32)
        aux = both[FEAT:FEAT + AUX]
        row = lax.broadcasted_iota(jnp.int32, (AUX, CHIP), 0)
        swapped = jnp.where(row < 3, 1.0, jnp.where(row < 6, pltpu.roll(aux, 3, 0), 0.0))
        cpm[h] = jnp.concatenate([hi, mid, scaled - hi - mid, swapped], axis=0).T.astype(BF)
        cv[h] = both[FEAT + AUX:].astype(BF)

    def halves(h):
        for half in range(2):
            arrived(cbuf.at[h, half], crecv.at[h, half])

    def cross(step, b):
        h, lb = tile_of(step, b)
        m[b] = jnp.maximum(jnp.dot(cpm[h], rw[lb], preferred_element_type=F32), 1e-30)

    def entries(b):
        d = m[b]
        t = d * lax.rsqrt(d)
        e = jnp.exp2(t * (-math.sqrt(3.0) * math.log2(math.e)))
        p = t + math.sqrt(0.75)
        return ((p * p + 0.25) * e).astype(BF)

    def products(step, b, kern):
        h, lb = tile_of(step, b)
        mine = jnp.where(h >= FULL, 1, 0)
        left, right = weights(h, lb)
        part = jnp.dot(cv[h], kern, preferred_element_type=F32)
        yr[2 * lb] += part[:, :128] * left
        yr[2 * lb + 1] += part[:, 128:] * right
        part = lax.dot_general(rv[mine, lb], kern, (((1,), (1,)), ((), ())), preferred_element_type=F32)
        for tile in range(3):
            yc[h, tile] += part[:, tile * 128:(tile + 1) * 128]

    def send_rows(pair):
        slot = 2 * pair + core
        arrived(pbuf.at[pair], precv.at[pair])
        at = pl.ds(slot * 3, 3)
        yr[at] = yr[at] + pbuf[pair]

        @pl.when(slot > 0)
        def _():
            row_sum(slot, 0).start()
        row_sum(slot, 1).start()

    def send_columns(h):
        for c in range(2):
            if STEPS[0][h] == (0, 0):
                @pl.when(jnp.logical_or(core == 1, c == 1))
                def _():
                    column_sum(h, c).start()
            else:
                column_sum(h, c).start()

    arrived(rbuf.at[0, other], hrecv)

    @pl.when(core == 0)
    def _():
        across(0).start()
        cbuf[3] = rbuf[0]

    @pl.when(core == 1)
    def _():
        halves(3)
        for taker, h in RELAYED:
            relay(taker, h).start()

    pass_even(1)
    pass_odd(0)
    pass_even(2)
    pass_odd(1)
    collect(0)
    halves(0)

    def first(i, _):
        column(3 * i)
        return 0

    lax.fori_loop(0, 2, first, 0)
    for b in range(COLS):
        cross(0, b)

    def work(step, _):
        later = step + 1

        @pl.when(later <= 5)
        def _():
            pass_even(later + 2)

        @pl.when(later <= 6)
        def _():
            pass_odd(later + 1)

        @pl.when(among(later, (1, 2, 3, 4, 14, 16, 18)))
        def _():
            collect(jnp.where(later <= 4, later, (later - 4) // 2))

        @pl.when(later == 5)
        def _():
            @pl.when(core == 0)
            def _():
                halves(1)

            @pl.when(core == 1)
            def _():
                arrived(cbuf.at[1], lrecv.at[1])
            last_relay().start()
            arrived(cbuf.at[2], lrecv.at[2])

            def middle(h, _):
                column(h)
                return 0
            lax.fori_loop(1, 3, middle, 0)

        @pl.when(later == 11)
        def _():
            arrived(cbuf.at[4], lrecv.at[4])
            column(4)

        before, after = jnp.maximum(step - 1, 0), jnp.minimum(step + 1, WORK - 1)
        for b in range(COLS):
            kern = entries(b)
            cross(after, b)
            products(before, b, k[b])
            k[b] = kern

        for when, pairs in ((12, (0,)), (13, (1, 2)), (14, (3,)), (15, (4,)), (17, (5,)), (19, (6,))):
            @pl.when(step == when)
            def _():
                for pair in pairs:
                    trade(pair).start()

        for when, pairs in ((13, (0,)), (14, (1, 2)), (15, (3,)), (16, (4,)), (18, (5,))):
            @pl.when(step == when)
            def _():
                for pair in pairs:
                    send_rows(pair)

        for when, h in ((6, 3), (14, 4)):
            @pl.when(step == when)
            def _():
                send_columns(h)
        return 0

    lax.fori_loop(0, WORK, work, 0)
    for b in range(COLS):
        products(WORK - 1, b, k[b])
    trade(7).start()
    for h in (2, 1, 0):
        send_columns(h)
    send_rows(6)
    send_rows(7)

    @pl.when(core == 0)
    def _():
        ybuf[0] = yr[0:2]
        zbuf[0, 3] = yc[3, 0:2]

    @pl.when(core == 1)
    def _():
        arrived(ybuf.at[0], yrecv.at[0])
        arrived(zbuf.at[0, 3], zrecv.at[0, 3])

    def add_rows(slot, total):
        arrived(ybuf.at[slot], yrecv.at[slot])
        return total + ybuf[slot]

    total = lax.fori_loop(1, PLACES, add_rows, ybuf[0] + zbuf[0, 3])
    for h in (3, 4, 2, 1, 0):
        for taker in range(2):
            if STEPS[taker][h] != (0, 0):
                arrived(zbuf.at[taker, h], zrecv.at[taker, h])
                total = total + zbuf[taker, h]
    total = total * scale
    main = jnp.where(core == 0, total[0], total[1])
    tail = jnp.where(core == 0, total[1], pltpu.roll(total[0], 64, 1))
    out[:, 0:128] = main
    out[:, 128:OWN] = tail[:, 0:64]

    share().wait_send()
    last_relay().wait_send()
    for taker, h in DIRECT:
        column_copy(taker, h).wait_send()

    @pl.when(core == 1)
    def _():
        for taker, h in RELAYED:
            relay(taker, h).wait_send()

    @pl.when(core == 0)
    def _():
        across(0).wait_send()

    @pl.loop(1, PLACES // 2)
    def _(j):
        row_copy(j).wait_send()

        @pl.when(core == j % 2)
        def _():
            forward(2 * j).wait_send()
            across(j).wait_send()

    @pl.loop(0, PLACES // 2)
    def _(j):
        @pl.when(core == (j + xl) % 2)
        def _():
            forward(2 * j + 1).wait_send()
        trade(j).wait_send()

        @pl.when(2 * j + core > 0)
        def _():
            row_sum(2 * j + core, 0).wait_send()
        row_sum(2 * j + core, 1).wait_send()

    for h in range(COLS):
        for c in range(2):
            if STEPS[0][h] == (0, 0):
                @pl.when(jnp.logical_or(core == 1, c == 1))
                def _():
                    column_sum(h, c).wait_send()
            else:
                column_sum(h, c).wait_send()


def on_device(points, probes):
    total = points.shape[1] * lax.axis_size("loop") * lax.axis_size("grp")
    vmem, dma = pltpu.VMEM, pltpu.SemaphoreType.DMA
    return pl.pallas_call(
        lambda *refs: kernel(float(total) ** (-0.5), *refs),
        out_shape=jax.ShapeDtypeStruct((PROBES, OWN), F32),
        in_specs=[pl.BlockSpec(memory_space=vmem)] * 2,
        out_specs=pl.BlockSpec(memory_space=vmem),
        scratch_shapes=[
            vmem((FOLD, 128), BF),
            vmem((PLACES, 2, FOLD, 128), BF),
            vmem((COLS, 2, FOLD, 128), BF),
            vmem((COLS, CHIP, DEPTH), BF),
            vmem((COLS, PROBES, CHIP), BF),
            vmem((BLOCKS, DEPTH, LANES), BF),
            vmem((2, BLOCKS, PROBES, LANES), BF),
            vmem((PLACES * 3, PROBES, 128), F32),
            vmem((COLS, 3, PROBES, 128), F32),
            vmem((PLACES // 2, 3, PROBES, 128), F32),
            vmem((PLACES, 2, PROBES, 128), F32),
            vmem((2, COLS, 2, PROBES, 128), F32),
            vmem((COLS, CHIP, LANES), F32),
            vmem((COLS, CHIP, LANES), BF),
            dma, dma, dma((PLACES // 2,)), dma((PLACES // 2, 2)), dma((PLACES // 2,)), dma((PLACES,)),
            dma((PLACES,)), dma((PLACES,)), dma((2, COLS)), dma((COLS, 2)), dma, dma((COLS,)),
            dma((PLACES // 2,)), dma((PLACES // 2,)), dma((PLACES, 2)), dma((PLACES,)), dma((COLS, 2)), dma((2, COLS)),
        ],
        compiler_params=pltpu.CompilerParams(
            collective_id=0, has_side_effects=True, vmem_limit_bytes=40 * 1024 * 1024
        ),
        name="matern_product",
    )(points, probes)


def solution(mesh):
    specs = P(None, ("loop", "grp"))
    return jax.shard_map(on_device, mesh=mesh, in_specs=(specs, specs), out_specs=specs, check_vma=False)
```

```python
import math

import jax
import jax.numpy as jnp
from jax import lax
from jax.experimental import pallas as pl
from jax.experimental.pallas import tpu as pltpu
from jax.sharding import PartitionSpec as P

MESH = pl.DeviceIdType.MESH
BF = jnp.bfloat16
F32 = jnp.float32
FEAT, PROBES, OWN = 64, 16, 192
AUX = 16
ROWS = FEAT + AUX + PROBES
FOLD = ROWS + ROWS // 2
DEPTH = 3 * FEAT + AUX
PLACES = 16
CHIP = 2 * OWN
LANES = 256
BLOCKS = PLACES * CHIP // LANES
STEPS = (((0, 1), (0, 6), (1, 7), (0, 0), (1, 4)),
         ((0, 3), (1, 2), (1, 5), (1, 0), (0, 4)))
FULL, COLS = 3, 5
DIRECT = ((1, 3), (0, 0), (1, 0), (0, 1))
RELAYED = ((1, 1), (0, 2), (1, 2))
NEAR = 9
BOTH = 14
WORK = (BOTH * COLS + (BLOCKS - BOTH) * FULL) // COLS


def device(xh, z, place, core):
    return ((z // 4 * 4 + xh * 2 + place % 2) * 2 + core, place // 2 * 4 + z % 4)


def tile_of(step, b):
    flat = step * COLS + b
    two, three = flat - 2 * NEAR, flat - 4 * NEAR
    four = three - COLS * (BOTH - NEAR)
    rest = four - NEAR
    all5 = jnp.maximum(three, 0) % 5
    all5 = jnp.where(all5 == 1, 3, jnp.where(jnp.logical_or(all5 == 2, all5 == 3), all5 - 1, all5))
    h = jnp.where(rest < 0, 4, rest % 3)
    h = jnp.where(three < 0, two % 2 + 1, jnp.where(four < 0, all5, h))
    lb = jnp.where(rest < 0, four, BOTH + rest // 3)
    lb = jnp.where(three < 0, two // 2, jnp.where(four < 0, NEAR + three // 5, lb))
    return jnp.where(two < 0, flat % 2 * 3, h), jnp.where(two < 0, flat // 2, lb)


def chip_step(pos):
    step = jnp.where(pos < 3, 2 * pos, jnp.where(pos < 10, 2 * pos - 5, pos - 1))
    step = jnp.where(pos == 4, 6, jnp.where(pos == 5, 3, jnp.where(pos == 6, 5, step)))
    step = jnp.where(pos == 7, 8, jnp.where(pos == 8, 7, jnp.where(pos == 9, 14, step)))
    return jnp.where(pos == 15, 15, step)


def weights(h, lb):
    mine = h >= FULL
    left = jnp.where(jnp.logical_and(mine, among(lb, (0, 1, 11))), 0.5, 1.0)
    right = jnp.where(jnp.logical_and(mine, among(lb, (0, 10, 11))), 0.5, 1.0)
    right = jnp.where(jnp.logical_and(mine, lb == 13), 0.0, right)
    return left, right


def among(value, options):
    hit = value == options[0]
    for option in options[1:]:
        hit = jnp.logical_or(hit, value == option)
    return hit


def tiles_of(halves):
    first, second = halves[0].astype(F32), halves[1].astype(F32)
    low = lax.broadcasted_iota(jnp.int32, (ROWS // 2, 128), 1) < 64
    f0, f1 = first[ROWS:], second[ROWS:]
    top = jnp.where(low, f0, pltpu.roll(f1, 64, 1))
    bottom = jnp.where(low, pltpu.roll(f0, 64, 1), f1)
    return first[:ROWS], jnp.concatenate([top, bottom], axis=0), second[:ROWS]


def kernel(scale, points, probes, out, pts, prb, own, rbuf, cbuf, cpm, cv, rw, rv, yr, yc, pbuf, ybuf, zbuf, m, k,
           hsend, hrecv, asend, arecv, rsend, rrecv, xsend, xrecv, fsend, frecv, csend, crecv, lsend, lrecv, psend, precv, ysend, yrecv,
           zsend, zrecv, isem):
    loop, grp = lax.axis_index("loop"), lax.axis_index("grp")
    core, x, z = loop % 2, (loop // 2) % 4, loop // 8 * 4 + grp % 4
    other = 1 - core
    xh, xl, place = x // 2, x % 2, grp // 4 * 2 + x % 2
    sibling = device(xh, z, place, other)

    def chosen(h):
        (ax, az), (bx, bz) = STEPS[0][h], STEPS[1][h]
        return jnp.where(core == 0, ax, bx), jnp.where(core == 0, az, bz)

    barrier = pltpu.get_barrier_semaphore()
    pl.semaphore_signal(barrier, inc=1, device_id=sibling, device_id_type=MESH)

    @pl.loop(1, 16)
    def _(step):
        for c in range(2):
            pl.semaphore_signal(barrier, inc=1, device_id=device(xh, z, (place + step) % PLACES, c), device_id_type=MESH)
            pl.semaphore_signal(barrier, inc=1, device_id=device((xh + step // 8) % 2, (z + step) % 8, place, c), device_id_type=MESH)

    copies = [pltpu.make_async_copy(points, pts, isem.at[0]), pltpu.make_async_copy(probes, prb, isem.at[1])]
    for copy in copies:
        copy.start()
    yr[...] = jnp.zeros_like(yr)
    yc[...] = jnp.zeros_like(yc)
    k[...] = jnp.zeros_like(k)
    for copy in copies:
        copy.wait()

    wide = pts[...].astype(F32)
    n = jnp.sum(wide * wide, axis=0, keepdims=True) * (5.0 / 3.0)
    hi = n.astype(BF).astype(F32)
    mid = (n - hi).astype(BF).astype(F32)
    lo = n - hi - mid
    row = lax.broadcasted_iota(jnp.int32, (AUX, OWN), 0)
    aux = jnp.where(row == 0, hi, jnp.where(row == 1, mid, jnp.where(row == 2, lo, jnp.where(row < 6, 1.0, 0.0))))
    chunk = jnp.concatenate([wide, aux, prb[...].astype(F32)], axis=0)
    own[0:ROWS, :] = chunk[:, :128].astype(BF)
    tail = chunk[:, 128:]
    own[ROWS:FOLD, :] = jnp.concatenate([tail[:ROWS // 2], tail[ROWS // 2:]], axis=1).astype(BF)
    rbuf[0, core] = own[...]

    pl.semaphore_wait(barrier, 1 + 15 * 4)

    def share():
        return pltpu.make_async_remote_copy(
            src_ref=own, dst_ref=rbuf.at[0, core], send_sem=hsend, recv_sem=hrecv,
            device_id=sibling, device_id_type=MESH)

    def row_copy(j):
        return pltpu.make_async_remote_copy(
            src_ref=own, dst_ref=rbuf.at[2 * j, core], send_sem=rsend.at[j], recv_sem=rrecv.at[j, core],
            device_id=device(xh, z, (place - 2 * j + PLACES) % PLACES, j % 2), device_id_type=MESH)

    def across(j):
        slot = jnp.where(xl == 1, 2 * j + 1, (2 * j + 15) % PLACES)
        return pltpu.make_async_remote_copy(
            src_ref=rbuf.at[2 * j], dst_ref=rbuf.at[slot], send_sem=xsend.at[j], recv_sem=xrecv.at[slot],
            device_id=device(xh, z, place + 1 - 2 * xl, core), device_id_type=MESH)

    def around():
        return pltpu.make_async_remote_copy(
            src_ref=rbuf.at[12], dst_ref=rbuf.at[8], send_sem=asend, recv_sem=arecv,
            device_id=device(xh, z, (place + 4) % PLACES, 0), device_id_type=MESH)

    def forward(slot):
        return pltpu.make_async_remote_copy(
            src_ref=rbuf.at[slot], dst_ref=rbuf.at[slot], send_sem=fsend.at[slot], recv_sem=frecv.at[slot],
            device_id=sibling, device_id_type=MESH)

    def column_copy(taker, h):
        dx, dz = STEPS[taker][h]
        return pltpu.make_async_remote_copy(
            src_ref=own, dst_ref=cbuf.at[h, core], send_sem=csend.at[taker, h], recv_sem=crecv.at[h, core],
            device_id=device((xh - dx + 2) % 2, (z - dz + 8) % 8, place, taker), device_id_type=MESH)

    def relay(taker, h):
        return pltpu.make_async_remote_copy(
            src_ref=cbuf.at[3], dst_ref=cbuf.at[h], send_sem=csend.at[taker, h], recv_sem=lrecv.at[h],
            device_id=device(xh, (z - STEPS[taker][h][1] + 8) % 8, place, taker), device_id_type=MESH)

    def last_relay():
        return pltpu.make_async_remote_copy(
            src_ref=cbuf.at[1], dst_ref=cbuf.at[4], send_sem=lsend, recv_sem=lrecv.at[4],
            device_id=device(xh, (z + jnp.where(core == 0, 2, 6)) % 8, place, other), device_id_type=MESH)

    def trade(pair):
        return pltpu.make_async_remote_copy(
            src_ref=yr.at[pl.ds((2 * pair + other) * 3, 3)], dst_ref=pbuf.at[pair], send_sem=psend.at[pair], recv_sem=precv.at[pair],
            device_id=sibling, device_id_type=MESH)

    def row_sum(pos, c):
        return pltpu.make_async_remote_copy(
            src_ref=yr.at[pl.ds(pos * 3 + c, 2)], dst_ref=ybuf.at[pos],
            send_sem=ysend.at[pos, c], recv_sem=yrecv.at[pos],
            device_id=device(xh, z, (place + chip_step(pos)) % PLACES, c), device_id_type=MESH)

    def column_sum(h, c):
        dx, dz = chosen(h)
        return pltpu.make_async_remote_copy(
            src_ref=yc.at[h, pl.ds(c, 2)], dst_ref=zbuf.at[core, h],
            send_sem=zsend.at[h, c], recv_sem=zrecv.at[core, h],
            device_id=device((xh + dx) % 2, (z + dz) % 8, place, c), device_id_type=MESH)

    def arrived(dst, sem):
        pltpu.make_async_remote_copy(
            src_ref=dst, dst_ref=dst, send_sem=fsend.at[0], recv_sem=sem, device_id=sibling, device_id_type=MESH).wait_recv()

    share().start()
    row_copy(1).start()
    column_copy(1, 3).start()
    column_copy(0, 0).start()
    row_copy(2).start()
    column_copy(1, 0).start()
    row_copy(3).start()
    row_copy(6).start()
    column_copy(0, 1).start()
    for j in (7, 5):
        row_copy(j).start()

    def pass_even(j):
        @pl.when(core == j % 2)
        def _():
            if j == 4:
                arrived(rbuf.at[8], arecv)
            else:
                for half in range(2):
                    arrived(rbuf.at[2 * j, half], rrecv.at[j, half])
            if j == 6:
                around().start()
            forward(2 * j).start()
            across(j).start()

    def pass_odd(j):
        @pl.when(core == (j + xl) % 2)
        def _():
            arrived(rbuf.at[2 * j + 1], xrecv.at[2 * j + 1])
            forward(2 * j + 1).start()

    def collect(pair):
        for t in range(2):
            slot = chip_step(2 * pair + t)
            j, odd = slot // 2, slot % 2

            @pl.when(jnp.logical_and(slot > 0, core != (j + odd * xl) % 2))
            def _():
                arrived(rbuf.at[slot], frecv.at[slot])
        prepare(pair)

    def prepare(pair):
        six = tiles_of(rbuf[chip_step(2 * pair)]) + tiles_of(rbuf[chip_step(2 * pair + 1)])
        for b in range(3):
            block = jnp.concatenate([six[2 * b], six[2 * b + 1]], axis=1)
            lb = 3 * pair + b
            feat = block[:FEAT].astype(BF)
            for piece in range(3):
                rw[lb, piece * FEAT:(piece + 1) * FEAT, :] = feat
            rw[lb, 3 * FEAT:, :] = block[FEAT:FEAT + AUX].astype(BF)
            probes = block[FEAT + AUX:]
            left, right = weights(FULL, lb)
            lane = lax.broadcasted_iota(jnp.int32, (PROBES, LANES), 1)
            rv[0, lb] = probes.astype(BF)
            rv[1, lb] = (probes * jnp.where(lane < 128, left, right)).astype(BF)

    def column(h):
        both = jnp.concatenate(tiles_of(cbuf[h]), axis=1)
        scaled = both[:FEAT] * (-10.0 / 3.0)
        hi = scaled.astype(BF).astype(F32)
        mid = (scaled - hi).astype(BF).astype(F32)
        aux = both[FEAT:FEAT + AUX]
        row = lax.broadcasted_iota(jnp.int32, (AUX, CHIP), 0)
        swapped = jnp.where(row < 3, 1.0, jnp.where(row < 6, pltpu.roll(aux, 3, 0), 0.0))
        cpm[h] = jnp.concatenate([hi, mid, scaled - hi - mid, swapped], axis=0).T.astype(BF)
        cv[h] = both[FEAT + AUX:].astype(BF)

    def halves(h):
        for half in range(2):
            arrived(cbuf.at[h, half], crecv.at[h, half])

    def cross(step, b):
        h, lb = tile_of(step, b)
        m[b] = jnp.maximum(jnp.dot(cpm[h], rw[lb], preferred_element_type=F32), 1e-30)

    def entries(b):
        d = m[b]
        t = d * lax.rsqrt(d)
        e = jnp.exp2(t * (-math.sqrt(3.0) * math.log2(math.e)))
        p = t + math.sqrt(0.75)
        return ((p * p + 0.25) * e).astype(BF)

    def products(step, b, kern):
        h, lb = tile_of(step, b)
        mine = jnp.where(h >= FULL, 1, 0)
        left, right = weights(h, lb)
        part = jnp.dot(cv[h], kern, preferred_element_type=F32)
        yr[2 * lb] += part[:, :128] * left
        yr[2 * lb + 1] += part[:, 128:] * right
        part = lax.dot_general(rv[mine, lb], kern, (((1,), (1,)), ((), ())), preferred_element_type=F32)
        for tile in range(3):
            yc[h, tile] += part[:, tile * 128:(tile + 1) * 128]

    def send_rows(pair):
        slot = 2 * pair + core
        arrived(pbuf.at[pair], precv.at[pair])
        at = pl.ds(slot * 3, 3)
        yr[at] = yr[at] + pbuf[pair]

        @pl.when(slot > 0)
        def _():
            row_sum(slot, 0).start()
        row_sum(slot, 1).start()

    def send_columns(h):
        for c in range(2):
            if STEPS[0][h] == (0, 0):
                @pl.when(jnp.logical_or(core == 1, c == 1))
                def _():
                    column_sum(h, c).start()
            else:
                column_sum(h, c).start()

    arrived(rbuf.at[0, other], hrecv)

    @pl.when(core == 0)
    def _():
        across(0).start()
        cbuf[3] = rbuf[0]

    @pl.when(core == 1)
    def _():
        halves(3)
        for taker, h in RELAYED:
            relay(taker, h).start()

    pass_even(1)

    @pl.when(core == 0)
    def _():
        halves(1)
        last_relay().start()
    collect(0)
    halves(0)

    def first(i, _):
        column(3 * i)
        return 0

    lax.fori_loop(0, 2, first, 0)
    pass_even(2)
    for b in range(COLS):
        cross(0, b)

    def tiles(step):
        before, after = jnp.maximum(step - 1, 0), jnp.minimum(step + 1, WORK - 1)
        for b in range(COLS):
            kern = entries(b)
            cross(after, b)
            products(before, b, k[b])
            k[b] = kern

    def work(step, _):
        later = step + 1

        def arrivals(events):
            for when, evens, odds, pairs in events:
                @pl.when(later == when)
                def _():
                    for j in evens:
                        pass_even(j)
                    for j in odds:
                        pass_odd(j)
                    for pair in pairs:
                        collect(pair)

        @pl.when(later < 8)
        def _():
            arrivals(((1, (6,), (0,), (1,)), (2, (3,), (1,), (2,)), (3, (7,), (), ()), (4, (5,), (), ()), (5, (4,), (), ()),
                      (6, (), (2,), ()), (7, (), (), (3,))))

            @pl.when(later == 3)
            def _():
                @pl.when(core == 1)
                def _():
                    arrived(cbuf.at[1], lrecv.at[1])
                    last_relay().start()
                arrived(cbuf.at[2], lrecv.at[2])

                def middle(h, _):
                    column(h)
                    return 0
                lax.fori_loop(1, 3, middle, 0)

        @pl.when(later >= 8)
        def _():
            arrivals(((9, (), (3, 4, 5), ()), (10, (), (6, 7), (4,))))

            @pl.when(later == 8)
            def _():
                arrived(cbuf.at[4], lrecv.at[4])
                column(4)

        tiles(step)
        return 0

    def work_two(half, _):
        for when, pair in ((6, 5), (7, 6), (8, 7)):
            @pl.when(half == when)
            def _():
                collect(pair)

        tiles(2 * half)
        tiles(2 * half + 1)
        for when, trades, sends, chunks in ((5, (3,), (), ()), (6, (0,), (3,), (3,)), (7, (1, 2, 4), (0,), (4,)), (8, (5,), (1, 2, 4), ()),
                                            (9, (6,), (5,), ())):
            @pl.when(half == when)
            def _():
                for pair in trades:
                    trade(pair).start()
                for pair in sends:
                    send_rows(pair)
                for h in chunks:
                    send_columns(h)
        return 0

    lax.fori_loop(0, WORK // 2, work, 0)
    lax.fori_loop(WORK // 4, WORK // 2, work_two, 0)
    for b in range(COLS):
        products(WORK - 1, b, k[b])
    trade(7).start()
    for h in (2, 1, 0):
        send_columns(h)
    send_rows(6)
    send_rows(7)

    share().wait_send()
    last_relay().wait_send()
    for taker, h in DIRECT:
        column_copy(taker, h).wait_send()

    @pl.when(core == 1)
    def _():
        for taker, h in RELAYED:
            relay(taker, h).wait_send()

    @pl.when(core == 0)
    def _():
        across(0).wait_send()
        around().wait_send()

    @pl.loop(1, PLACES // 2)
    def _(j):
        @pl.when(j != 4)
        def _():
            row_copy(j).wait_send()

        @pl.when(core == j % 2)
        def _():
            forward(2 * j).wait_send()
            across(j).wait_send()

    @pl.loop(0, PLACES // 2)
    def _(j):
        @pl.when(core == (j + xl) % 2)
        def _():
            forward(2 * j + 1).wait_send()

    @pl.loop(0, PLACES // 2)
    def _(j):
        trade(j).wait_send()

        @pl.when(2 * j + core > 0)
        def _():
            row_sum(2 * j + core, 0).wait_send()
        row_sum(2 * j + core, 1).wait_send()

    for h in range(COLS):
        for c in range(2):
            if STEPS[0][h] == (0, 0):
                @pl.when(jnp.logical_or(core == 1, c == 1))
                def _():
                    column_sum(h, c).wait_send()
            else:
                column_sum(h, c).wait_send()

    @pl.when(core == 0)
    def _():
        ybuf[0] = yr[0:2]
        zbuf[0, 3] = yc[3, 0:2]

    @pl.when(core == 1)
    def _():
        arrived(ybuf.at[0], yrecv.at[0])
        arrived(zbuf.at[0, 3], zrecv.at[0, 3])

    def add_rows(slot, total):
        arrived(ybuf.at[slot], yrecv.at[slot])
        return total + ybuf[slot]

    total = lax.fori_loop(1, PLACES, add_rows, ybuf[0] + zbuf[0, 3])
    for h in (3, 4, 2, 1, 0):
        for taker in range(2):
            if STEPS[taker][h] != (0, 0):
                arrived(zbuf.at[taker, h], zrecv.at[taker, h])
                total = total + zbuf[taker, h]
    total = total * scale
    main = jnp.where(core == 0, total[0], total[1])
    tail = jnp.where(core == 0, total[1], pltpu.roll(total[0], 64, 1))
    out[:, 0:128] = main
    out[:, 128:OWN] = tail[:, 0:64]


def on_device(points, probes):
    total = points.shape[1] * lax.axis_size("loop") * lax.axis_size("grp")
    vmem, dma = pltpu.VMEM, pltpu.SemaphoreType.DMA
    return pl.pallas_call(
        lambda *refs: kernel(float(total) ** (-0.5), *refs),
        out_shape=jax.ShapeDtypeStruct((PROBES, OWN), F32),
        in_specs=[pl.BlockSpec(memory_space=pltpu.HBM)] * 2,
        out_specs=pl.BlockSpec(memory_space=vmem),
        scratch_shapes=[
            vmem((FEAT, OWN), BF),
            vmem((PROBES, OWN), BF),
            vmem((FOLD, 128), BF),
            vmem((PLACES, 2, FOLD, 128), BF),
            vmem((COLS, 2, FOLD, 128), BF),
            vmem((COLS, CHIP, DEPTH), BF),
            vmem((COLS, PROBES, CHIP), BF),
            vmem((BLOCKS, DEPTH, LANES), BF),
            vmem((2, BLOCKS, PROBES, LANES), BF),
            vmem((PLACES * 3, PROBES, 128), F32),
            vmem((COLS, 3, PROBES, 128), F32),
            vmem((PLACES // 2, 3, PROBES, 128), F32),
            vmem((PLACES, 2, PROBES, 128), F32),
            vmem((2, COLS, 2, PROBES, 128), F32),
            vmem((COLS, CHIP, LANES), F32),
            vmem((COLS, CHIP, LANES), BF),
            dma, dma, dma, dma, dma((PLACES // 2,)), dma((PLACES // 2, 2)), dma((PLACES // 2,)), dma((PLACES,)),
            dma((PLACES,)), dma((PLACES,)), dma((2, COLS)), dma((COLS, 2)), dma, dma((COLS,)),
            dma((PLACES // 2,)), dma((PLACES // 2,)), dma((PLACES, 2)), dma((PLACES,)), dma((COLS, 2)), dma((2, COLS)), dma((2,)),
        ],
        compiler_params=pltpu.CompilerParams(
            collective_id=0, has_side_effects=True, vmem_limit_bytes=40 * 1024 * 1024
        ),
        name="matern_product",
    )(points, probes)


def solution(mesh):
    specs = P(None, ("loop", "grp"))
    return jax.shard_map(on_device, mesh=mesh, in_specs=(specs, specs), out_specs=specs, check_vma=False)
```

```python
import math

import jax
import jax.numpy as jnp
from jax import lax
from jax.experimental import pallas as pl
from jax.experimental.pallas import tpu as pltpu
from jax.sharding import PartitionSpec as P

MESH = pl.DeviceIdType.MESH
BF = jnp.bfloat16
F32 = jnp.float32
FEAT, PROBES, OWN = 64, 16, 192
AUX = 16
ROWS = FEAT + AUX + PROBES
FOLD = ROWS + ROWS // 2
DEPTH = 3 * FEAT + AUX
PLACES = 16
CHIP = 2 * OWN
LANES = 256
BLOCKS = PLACES * CHIP // LANES
STEPS = (((0, 1), (0, 6), (1, 7), (0, 0), (1, 4)),
         ((0, 3), (1, 2), (1, 5), (1, 0), (0, 4)))
FULL, COLS = 3, 5
DIRECT = ((1, 3), (0, 0), (1, 0), (0, 1))
RELAYED = ((1, 1), (0, 2), (1, 2))
NEAR, NEXT = 9, 12
BOTH = 14
WORK = (BOTH * COLS + (BLOCKS - BOTH) * FULL) // COLS


def device(xh, z, place, core):
    return ((z // 4 * 4 + xh * 2 + place % 2) * 2 + core, place // 2 * 4 + z % 4)


def tile_of(step, b):
    flat = step * COLS + b
    two, three = flat - 2 * NEAR, flat - 4 * NEAR
    four = three - COLS * (NEXT - NEAR)
    five = four - NEAR
    rest = five - COLS * (BOTH - NEXT)
    turn = jnp.where(four < 0, three, five) % 5
    turn = jnp.where(turn == 1, 3, jnp.where(jnp.logical_or(turn == 2, turn == 3), turn - 1, turn))
    h = jnp.where(rest < 0, turn, rest % 3)
    h = jnp.where(jnp.logical_and(four >= 0, five < 0), 4, jnp.where(three < 0, two % 2 + 1, h))
    lb = jnp.where(rest < 0, NEXT + five // 5, BOTH + rest // 3)
    lb = jnp.where(four < 0, NEAR + three // 5, jnp.where(five < 0, four, lb))
    lb = jnp.where(three < 0, two // 2, lb)
    return jnp.where(two < 0, flat % 2 * 3, h), jnp.where(two < 0, flat // 2, lb)


def chip_step(pos):
    step = jnp.where(pos < 3, 2 * pos, jnp.where(pos < 10, 2 * pos - 5, pos - 1))
    step = jnp.where(pos == 4, 6, jnp.where(pos == 5, 3, jnp.where(pos == 6, 5, step)))
    step = jnp.where(pos == 7, 8, jnp.where(pos == 8, 7, jnp.where(pos == 9, 14, step)))
    return jnp.where(pos == 15, 15, step)


def weights(h, lb):
    mine = h >= FULL
    left = jnp.where(jnp.logical_and(mine, among(lb, (0, 1, 11))), 0.5, 1.0)
    right = jnp.where(jnp.logical_and(mine, among(lb, (0, 10, 11))), 0.5, 1.0)
    right = jnp.where(jnp.logical_and(mine, lb == 13), 0.0, right)
    return left, right


def among(value, options):
    hit = value == options[0]
    for option in options[1:]:
        hit = jnp.logical_or(hit, value == option)
    return hit


def tiles_of(halves):
    first, second = halves[0].astype(F32), halves[1].astype(F32)
    low = lax.broadcasted_iota(jnp.int32, (ROWS // 2, 128), 1) < 64
    f0, f1 = first[ROWS:], second[ROWS:]
    top = jnp.where(low, f0, pltpu.roll(f1, 64, 1))
    bottom = jnp.where(low, pltpu.roll(f0, 64, 1), f1)
    return first[:ROWS], jnp.concatenate([top, bottom], axis=0), second[:ROWS]


def kernel(scale, points, probes, out, pts, prb, own, rbuf, cbuf, cpm, cv, rw, rv, yr, yc, pbuf, ybuf, zbuf, m, k,
           hsend, hrecv, asend, arecv, rsend, rrecv, xsend, xrecv, fsend, frecv, csend, crecv, lsend, lrecv, psend, precv, ysend, yrecv,
           zsend, zrecv, isem):
    loop, grp = lax.axis_index("loop"), lax.axis_index("grp")
    core, x, z = loop % 2, (loop // 2) % 4, loop // 8 * 4 + grp % 4
    other = 1 - core
    xh, xl, place = x // 2, x % 2, grp // 4 * 2 + x % 2
    sibling = device(xh, z, place, other)

    def chosen(h):
        (ax, az), (bx, bz) = STEPS[0][h], STEPS[1][h]
        return jnp.where(core == 0, ax, bx), jnp.where(core == 0, az, bz)

    barrier = pltpu.get_barrier_semaphore()
    pl.semaphore_signal(barrier, inc=1, device_id=sibling, device_id_type=MESH)

    @pl.loop(1, 16)
    def _(step):
        for c in range(2):
            pl.semaphore_signal(barrier, inc=1, device_id=device(xh, z, (place + step) % PLACES, c), device_id_type=MESH)
            pl.semaphore_signal(barrier, inc=1, device_id=device((xh + step // 8) % 2, (z + step) % 8, place, c), device_id_type=MESH)

    copies = [pltpu.make_async_copy(points, pts, isem.at[0]), pltpu.make_async_copy(probes, prb, isem.at[1])]
    for copy in copies:
        copy.start()
    yr[...] = jnp.zeros_like(yr)
    yc[...] = jnp.zeros_like(yc)
    k[...] = jnp.zeros_like(k)
    for copy in copies:
        copy.wait()

    wide = pts[...].astype(F32)
    n = jnp.sum(wide * wide, axis=0, keepdims=True) * (5.0 / 3.0)
    hi = n.astype(BF).astype(F32)
    mid = (n - hi).astype(BF).astype(F32)
    lo = n - hi - mid
    row = lax.broadcasted_iota(jnp.int32, (AUX, OWN), 0)
    aux = jnp.where(row == 0, hi, jnp.where(row == 1, mid, jnp.where(row == 2, lo, jnp.where(row < 6, 1.0, 0.0))))
    chunk = jnp.concatenate([wide, aux, prb[...].astype(F32)], axis=0)
    own[0:ROWS, :] = chunk[:, :128].astype(BF)
    tail = chunk[:, 128:]
    own[ROWS:FOLD, :] = jnp.concatenate([tail[:ROWS // 2], tail[ROWS // 2:]], axis=1).astype(BF)
    rbuf[0, core] = own[...]

    pl.semaphore_wait(barrier, 1 + 15 * 4)

    def share():
        return pltpu.make_async_remote_copy(
            src_ref=own, dst_ref=rbuf.at[0, core], send_sem=hsend, recv_sem=hrecv,
            device_id=sibling, device_id_type=MESH)

    def row_copy(j):
        return pltpu.make_async_remote_copy(
            src_ref=own, dst_ref=rbuf.at[2 * j, core], send_sem=rsend.at[j], recv_sem=rrecv.at[j // 2, core],
            device_id=device(xh, z, (place - 2 * j + PLACES) % PLACES, j % 2), device_id_type=MESH)

    def across(j):
        slot = jnp.where(xl == 1, 2 * j + 1, (2 * j + 15) % PLACES)
        return pltpu.make_async_remote_copy(
            src_ref=rbuf.at[2 * j], dst_ref=rbuf.at[slot], send_sem=xsend.at[j // 2], recv_sem=xrecv.at[slot // 4],
            device_id=device(xh, z, place + 1 - 2 * xl, core), device_id_type=MESH)

    def around():
        return pltpu.make_async_remote_copy(
            src_ref=rbuf.at[12], dst_ref=rbuf.at[8], send_sem=asend, recv_sem=arecv,
            device_id=device(xh, z, (place + 4) % PLACES, 0), device_id_type=MESH)

    def forward(slot):
        return pltpu.make_async_remote_copy(
            src_ref=rbuf.at[slot], dst_ref=rbuf.at[slot], send_sem=fsend.at[slot % 2 * 4 + slot // 4], recv_sem=frecv.at[slot % 2 * 4 + slot // 4],
            device_id=sibling, device_id_type=MESH)

    def column_copy(taker, h):
        dx, dz = STEPS[taker][h]
        return pltpu.make_async_remote_copy(
            src_ref=own, dst_ref=cbuf.at[h, core], send_sem=csend.at[taker, h], recv_sem=crecv.at[h, core],
            device_id=device((xh - dx + 2) % 2, (z - dz + 8) % 8, place, taker), device_id_type=MESH)

    def relay(taker, h):
        return pltpu.make_async_remote_copy(
            src_ref=cbuf.at[3], dst_ref=cbuf.at[h], send_sem=csend.at[taker, h], recv_sem=lrecv.at[h // 2],
            device_id=device(xh, (z - STEPS[taker][h][1] + 8) % 8, place, taker), device_id_type=MESH)

    def last_relay():
        return pltpu.make_async_remote_copy(
            src_ref=cbuf.at[1], dst_ref=cbuf.at[4], send_sem=lsend, recv_sem=lrecv.at[2],
            device_id=device(xh, (z + jnp.where(core == 0, 2, 6)) % 8, place, other), device_id_type=MESH)

    def trade(pair):
        return pltpu.make_async_remote_copy(
            src_ref=yr.at[pl.ds((2 * pair + other) * 3, 3)], dst_ref=pbuf.at[pair], send_sem=psend.at[pair], recv_sem=precv.at[pair],
            device_id=sibling, device_id_type=MESH)

    def row_sum(pos, c):
        return pltpu.make_async_remote_copy(
            src_ref=yr.at[pl.ds(pos * 3 + c, 2)], dst_ref=ybuf.at[pos],
            send_sem=ysend.at[pos // 2, c], recv_sem=yrecv.at[pos],
            device_id=device(xh, z, (place + chip_step(pos)) % PLACES, c), device_id_type=MESH)

    def column_sum(h, c):
        dx, dz = chosen(h)
        return pltpu.make_async_remote_copy(
            src_ref=yc.at[h, pl.ds(c, 2)], dst_ref=zbuf.at[core, h],
            send_sem=zsend.at[h, c], recv_sem=zrecv.at[core, h],
            device_id=device((xh + dx) % 2, (z + dz) % 8, place, c), device_id_type=MESH)

    def arrived(dst, sem):
        pltpu.make_async_remote_copy(
            src_ref=dst, dst_ref=dst, send_sem=fsend.at[0], recv_sem=sem, device_id=sibling, device_id_type=MESH).wait_recv()

    share().start()
    row_copy(1).start()
    column_copy(1, 3).start()
    column_copy(0, 0).start()
    row_copy(2).start()
    column_copy(1, 0).start()
    row_copy(3).start()
    row_copy(6).start()
    column_copy(0, 1).start()
    for j in (7, 5):
        row_copy(j).start()

    def pass_even(j):
        @pl.when(core == j % 2)
        def _():
            if j == 4:
                arrived(rbuf.at[8], arecv)
            else:
                for half in range(2):
                    arrived(rbuf.at[2 * j, half], rrecv.at[j // 2, half])
            if j == 6:
                around().start()
            forward(2 * j).start()
            across(j).start()

    def pass_odd(j):
        @pl.when(core == (j + xl) % 2)
        def _():
            arrived(rbuf.at[2 * j + 1], xrecv.at[j // 2])
            forward(2 * j + 1).start()

    def collect(pair):
        for t in range(2):
            slot = chip_step(2 * pair + t)
            j, odd = slot // 2, slot % 2

            @pl.when(jnp.logical_and(slot > 0, core != (j + odd * xl) % 2))
            def _():
                arrived(rbuf.at[slot], frecv.at[slot % 2 * 4 + slot // 4])
        prepare(pair)

    def prepare(pair):
        six = tiles_of(rbuf[chip_step(2 * pair)]) + tiles_of(rbuf[chip_step(2 * pair + 1)])
        for b in range(3):
            block = jnp.concatenate([six[2 * b], six[2 * b + 1]], axis=1)
            lb = 3 * pair + b
            feat = block[:FEAT].astype(BF)
            for piece in range(3):
                rw[lb, piece * FEAT:(piece + 1) * FEAT, :] = feat
            rw[lb, 3 * FEAT:, :] = block[FEAT:FEAT + AUX].astype(BF)
            probes = block[FEAT + AUX:]
            left, right = weights(FULL, lb)
            lane = lax.broadcasted_iota(jnp.int32, (PROBES, LANES), 1)
            rv[0, lb] = probes.astype(BF)
            rv[1, lb] = (probes * jnp.where(lane < 128, left, right)).astype(BF)

    def column(h):
        both = jnp.concatenate(tiles_of(cbuf[h]), axis=1)
        scaled = both[:FEAT] * (-10.0 / 3.0)
        hi = scaled.astype(BF).astype(F32)
        mid = (scaled - hi).astype(BF).astype(F32)
        aux = both[FEAT:FEAT + AUX]
        row = lax.broadcasted_iota(jnp.int32, (AUX, CHIP), 0)
        swapped = jnp.where(row < 3, 1.0, jnp.where(row < 6, pltpu.roll(aux, 3, 0), 0.0))
        cpm[h] = jnp.concatenate([hi, mid, scaled - hi - mid, swapped], axis=0).T.astype(BF)
        cv[h] = both[FEAT + AUX:].astype(BF)

    def halves(h):
        for half in range(2):
            arrived(cbuf.at[h, half], crecv.at[h, half])

    def cross(step, b):
        h, lb = tile_of(step, b)
        m[b] = jnp.maximum(jnp.dot(cpm[h], rw[lb], preferred_element_type=F32), 1e-30)

    def entries(b):
        d = m[b]
        t = d * lax.rsqrt(d)
        e = jnp.exp2(t * (-math.sqrt(3.0) * math.log2(math.e)))
        p = t + math.sqrt(0.75)
        return ((p * p + 0.25) * e).astype(BF)

    def products(step, b, kern):
        h, lb = tile_of(step, b)
        mine = jnp.where(h >= FULL, 1, 0)
        left, right = weights(h, lb)
        part = jnp.dot(cv[h], kern, preferred_element_type=F32)
        yr[2 * lb] += part[:, :128] * left
        yr[2 * lb + 1] += part[:, 128:] * right
        part = lax.dot_general(rv[mine, lb], kern, (((1,), (1,)), ((), ())), preferred_element_type=F32)
        for tile in range(3):
            yc[h, tile] += part[:, tile * 128:(tile + 1) * 128]

    def send_rows(pair):
        slot = 2 * pair + core
        arrived(pbuf.at[pair], precv.at[pair])
        at = pl.ds(slot * 3, 3)
        yr[at] = yr[at] + pbuf[pair]

        @pl.when(slot > 0)
        def _():
            row_sum(slot, 0).start()
        row_sum(slot, 1).start()

    def send_columns(h):
        for c in range(2):
            if STEPS[0][h] == (0, 0):
                @pl.when(jnp.logical_or(core == 1, c == 1))
                def _():
                    column_sum(h, c).start()
            else:
                column_sum(h, c).start()

    arrived(rbuf.at[0, other], hrecv)

    @pl.when(core == 0)
    def _():
        across(0).start()
        cbuf[3] = rbuf[0]

    @pl.when(core == 1)
    def _():
        halves(3)
        for taker, h in RELAYED:
            relay(taker, h).start()

    pass_even(1)

    @pl.when(core == 0)
    def _():
        halves(1)
        last_relay().start()
    collect(0)
    halves(0)

    def first(i, _):
        column(3 * i)
        return 0

    lax.fori_loop(0, 2, first, 0)
    pass_even(2)
    for b in range(COLS):
        cross(0, b)

    def tiles(step):
        before, after = jnp.maximum(step - 1, 0), jnp.minimum(step + 1, WORK - 1)
        for b in range(COLS):
            kern = entries(b)
            cross(after, b)
            products(before, b, k[b])
            k[b] = kern

    def arrivals(count, events):
        for when, evens, odds, pairs in events:
            @pl.when(count == when)
            def _():
                for j in evens:
                    pass_even(j)
                for j in odds:
                    pass_odd(j)
                for pair in pairs:
                    collect(pair)

    def work(step, _):
        arrivals(step, ((0, (6,), (0,), (1,)), (1, (3,), (1,), (2,))))
        tiles(step)
        return 0

    def work_two(half, _):
        @pl.when(half < 5)
        def _():
            arrivals(half, ((1, (7, 5), (), ()), (2, (4,), (2,), ()), (3, (), (), (3,)), (4, (), (3, 4, 5, 6, 7), ())))

            @pl.when(half == 1)
            def _():
                @pl.when(core == 1)
                def _():
                    arrived(cbuf.at[1], lrecv.at[0])
                    last_relay().start()
                arrived(cbuf.at[2], lrecv.at[1])

                def middle(h, _):
                    column(h)
                    return 0
                lax.fori_loop(1, 3, middle, 0)

            @pl.when(half == 3)
            def _():
                arrived(cbuf.at[4], lrecv.at[2])
                column(4)

        @pl.when(half >= 5)
        def _():
            arrivals(half, ((5, (), (), (4,)), (6, (), (), (5,)), (7, (), (), (6,)), (8, (), (), (7,))))

        tiles(2 * half)
        tiles(2 * half + 1)

        @pl.when(half >= 5)
        def _():
            for when, trades, sends, chunks in ((5, (3, 0), (), ()), (6, (1, 2), (3, 0), ()), (7, (4,), (1, 2), (3, 4)),
                                                (8, (5,), (4,), ()), (9, (6,), (5,), ())):
                @pl.when(half == when)
                def _():
                    for pair in trades:
                        trade(pair).start()
                    for pair in sends:
                        send_rows(pair)
                    for h in chunks:
                        send_columns(h)
        return 0

    lax.fori_loop(0, 2, work, 0)
    lax.fori_loop(1, WORK // 2, work_two, 0)
    for b in range(COLS):
        products(WORK - 1, b, k[b])
    trade(7).start()
    for h in (2, 1, 0):
        send_columns(h)
    send_rows(6)
    send_rows(7)

    share().wait_send()
    last_relay().wait_send()
    for taker, h in DIRECT:
        column_copy(taker, h).wait_send()

    @pl.when(core == 1)
    def _():
        for taker, h in RELAYED:
            relay(taker, h).wait_send()

    @pl.when(core == 0)
    def _():
        across(0).wait_send()
        around().wait_send()

    @pl.loop(1, PLACES // 2)
    def _(j):
        @pl.when(j != 4)
        def _():
            row_copy(j).wait_send()

        @pl.when(core == j % 2)
        def _():
            forward(2 * j).wait_send()
            across(j).wait_send()

    @pl.loop(0, PLACES // 2)
    def _(j):
        @pl.when(core == (j + xl) % 2)
        def _():
            forward(2 * j + 1).wait_send()

    @pl.loop(0, PLACES // 2)
    def _(j):
        trade(j).wait_send()

        @pl.when(2 * j + core > 0)
        def _():
            row_sum(2 * j + core, 0).wait_send()
        row_sum(2 * j + core, 1).wait_send()

    for h in range(COLS):
        for c in range(2):
            if STEPS[0][h] == (0, 0):
                @pl.when(jnp.logical_or(core == 1, c == 1))
                def _():
                    column_sum(h, c).wait_send()
            else:
                column_sum(h, c).wait_send()

    @pl.when(core == 0)
    def _():
        ybuf[0] = yr[0:2]
        zbuf[0, 3] = yc[3, 0:2]

    @pl.when(core == 1)
    def _():
        arrived(ybuf.at[0], yrecv.at[0])
        arrived(zbuf.at[0, 3], zrecv.at[0, 3])

    def add_rows(slot, total):
        arrived(ybuf.at[slot], yrecv.at[slot])
        return total + ybuf[slot]

    total = lax.fori_loop(1, PLACES, add_rows, ybuf[0] + zbuf[0, 3])
    for h in (3, 4, 2, 1, 0):
        for taker in range(2):
            if STEPS[taker][h] != (0, 0):
                arrived(zbuf.at[taker, h], zrecv.at[taker, h])
                total = total + zbuf[taker, h]
    total = total * scale
    main = jnp.where(core == 0, total[0], total[1])
    tail = jnp.where(core == 0, total[1], pltpu.roll(total[0], 64, 1))
    out[:, 0:128] = main
    out[:, 128:OWN] = tail[:, 0:64]


def on_device(points, probes):
    total = points.shape[1] * lax.axis_size("loop") * lax.axis_size("grp")
    vmem, dma = pltpu.VMEM, pltpu.SemaphoreType.DMA
    return pl.pallas_call(
        lambda *refs: kernel(float(total) ** (-0.5), *refs),
        out_shape=jax.ShapeDtypeStruct((PROBES, OWN), F32),
        in_specs=[pl.BlockSpec(memory_space=pltpu.HBM)] * 2,
        out_specs=pl.BlockSpec(memory_space=vmem),
        scratch_shapes=[
            vmem((FEAT, OWN), BF),
            vmem((PROBES, OWN), BF),
            vmem((FOLD, 128), BF),
            vmem((PLACES, 2, FOLD, 128), BF),
            vmem((COLS, 2, FOLD, 128), BF),
            vmem((COLS, CHIP, DEPTH), BF),
            vmem((COLS, PROBES, CHIP), BF),
            vmem((BLOCKS, DEPTH, LANES), BF),
            vmem((2, BLOCKS, PROBES, LANES), BF),
            vmem((PLACES * 3, PROBES, 128), F32),
            vmem((COLS, 3, PROBES, 128), F32),
            vmem((PLACES // 2, 3, PROBES, 128), F32),
            vmem((PLACES, 2, PROBES, 128), F32),
            vmem((2, COLS, 2, PROBES, 128), F32),
            vmem((COLS, CHIP, LANES), F32),
            vmem((COLS, CHIP, LANES), BF),
            dma, dma, dma, dma, dma((PLACES // 2,)), dma((PLACES // 4, 2)), dma((PLACES // 4,)), dma((PLACES // 4,)),
            dma((PLACES // 2,)), dma((PLACES // 2,)), dma((2, COLS)), dma((COLS, 2)), dma, dma((3,)),
            dma((PLACES // 2,)), dma((PLACES // 2,)), dma((PLACES // 2, 2)), dma((PLACES,)), dma((COLS, 2)), dma((2, COLS)), dma((2,)),
        ],
        compiler_params=pltpu.CompilerParams(
            collective_id=0, has_side_effects=True, vmem_limit_bytes=40 * 1024 * 1024
        ),
        name="matern_product",
    )(points, probes)


def solution(mesh):
    specs = P(None, ("loop", "grp"))
    return jax.shard_map(on_device, mesh=mesh, in_specs=(specs, specs), out_specs=specs, check_vma=False)
```

```python
import math

import jax
import jax.numpy as jnp
from jax import lax
from jax.experimental import pallas as pl
from jax.experimental.pallas import tpu as pltpu
from jax.sharding import PartitionSpec as P

MESH = pl.DeviceIdType.MESH
BF = jnp.bfloat16
F32 = jnp.float32
FEAT, PROBES, OWN = 64, 16, 192
AUX = 16
ROWS = FEAT + AUX + PROBES
FOLD = ROWS + ROWS // 2
DEPTH = 3 * FEAT + AUX
PLACES = 16
CHIP = 2 * OWN
LANES = 256
BLOCKS = PLACES * CHIP // LANES
STEPS = (((0, 1), (0, 6), (1, 7), (0, 0), (1, 4)),
         ((0, 3), (1, 2), (1, 5), (1, 0), (0, 4)))
FULL, COLS = 3, 5
DIRECT = ((1, 3), (0, 0), (1, 0), (0, 1))
RELAYED = ((1, 1), (0, 2), (1, 2))
NEAR, NEXT = 9, 12
BOTH = 14
WORK = (BOTH * COLS + (BLOCKS - BOTH) * FULL) // COLS


def device(xh, z, place, core):
    return ((z // 4 * 4 + xh * 2 + place % 2) * 2 + core, place // 2 * 4 + z % 4)


def tile_of(step, b):
    flat = step * COLS + b
    two, three = flat - 2 * NEAR, flat - 4 * NEAR
    four = three - COLS * (NEXT - NEAR)
    five = four - NEAR
    rest = five - COLS * (BOTH - NEXT)
    turn = jnp.where(four < 0, three, five) % 5
    turn = jnp.where(turn == 1, 3, jnp.where(jnp.logical_or(turn == 2, turn == 3), turn - 1, turn))
    h = jnp.where(rest < 0, turn, rest % 3)
    h = jnp.where(jnp.logical_and(four >= 0, five < 0), 4, jnp.where(three < 0, two % 2 + 1, h))
    lb = jnp.where(rest < 0, NEXT + five // 5, BOTH + rest // 3)
    lb = jnp.where(four < 0, NEAR + three // 5, jnp.where(five < 0, four, lb))
    lb = jnp.where(three < 0, two // 2, lb)
    return jnp.where(two < 0, flat % 2 * 3, h), jnp.where(two < 0, flat // 2, lb)


def chip_step(pos):
    step = jnp.where(pos < 3, 2 * pos, jnp.where(pos < 10, 2 * pos - 5, pos - 1))
    step = jnp.where(pos == 4, 6, jnp.where(pos == 5, 3, jnp.where(pos == 6, 5, step)))
    step = jnp.where(pos == 7, 8, jnp.where(pos == 8, 7, jnp.where(pos == 9, 14, step)))
    return jnp.where(pos == 15, 15, step)


def weights(h, lb):
    mine = h >= FULL
    left = jnp.where(jnp.logical_and(mine, among(lb, (0, 1, 11))), 0.5, 1.0)
    right = jnp.where(jnp.logical_and(mine, among(lb, (0, 10, 11))), 0.5, 1.0)
    right = jnp.where(jnp.logical_and(mine, lb == 13), 0.0, right)
    return left, right


def among(value, options):
    hit = value == options[0]
    for option in options[1:]:
        hit = jnp.logical_or(hit, value == option)
    return hit


def tiles_of(halves):
    first, second = halves[0].astype(F32), halves[1].astype(F32)
    low = lax.broadcasted_iota(jnp.int32, (ROWS // 2, 128), 1) < 64
    f0, f1 = first[ROWS:], second[ROWS:]
    top = jnp.where(low, f0, pltpu.roll(f1, 64, 1))
    bottom = jnp.where(low, pltpu.roll(f0, 64, 1), f1)
    return first[:ROWS], jnp.concatenate([top, bottom], axis=0), second[:ROWS]


def kernel(scale, points, probes, out, pts, prb, own, rbuf, cbuf, cpm, cv, rw, rv, yr, yc, pbuf, ybuf, zbuf, m, k,
           hsend, hrecv, asend, arecv, rsend, rrecv, xsend, xrecv, fsend, frecv, csend, crecv, lsend, lrecv, psend, precv, ysend, yrecv,
           zsend, zrecv, isem):
    loop, grp = lax.axis_index("loop"), lax.axis_index("grp")
    core, x, z = loop % 2, (loop // 2) % 4, loop // 8 * 4 + grp % 4
    other = 1 - core
    xh, xl, place = x // 2, x % 2, grp // 4 * 2 + x % 2
    sibling = device(xh, z, place, other)

    def chosen(h):
        (ax, az), (bx, bz) = STEPS[0][h], STEPS[1][h]
        return jnp.where(core == 0, ax, bx), jnp.where(core == 0, az, bz)

    barrier = pltpu.get_barrier_semaphore()
    pl.semaphore_signal(barrier, inc=1, device_id=sibling, device_id_type=MESH)

    @pl.loop(1, 16)
    def _(step):
        for c in range(2):
            pl.semaphore_signal(barrier, inc=1, device_id=device((xh + step // 8) % 2, (z + step) % 8, place, c), device_id_type=MESH)

    @pl.loop(1, 16)
    def _(step):
        for c in range(2):
            pl.semaphore_signal(barrier, inc=1, device_id=device(xh, z, (place + step) % PLACES, c), device_id_type=MESH)

    copies = [pltpu.make_async_copy(points, pts, isem.at[0]), pltpu.make_async_copy(probes, prb, isem.at[1])]
    for copy in copies:
        copy.start()
    yr[...] = jnp.zeros_like(yr)
    yc[...] = jnp.zeros_like(yc)
    k[...] = jnp.zeros_like(k)
    for copy in copies:
        copy.wait()

    wide = pts[...].astype(F32)
    n = jnp.sum(wide * wide, axis=0, keepdims=True) * (5.0 / 3.0)
    hi = n.astype(BF).astype(F32)
    mid = (n - hi).astype(BF).astype(F32)
    lo = n - hi - mid
    row = lax.broadcasted_iota(jnp.int32, (AUX, OWN), 0)
    aux = jnp.where(row == 0, hi, jnp.where(row == 1, mid, jnp.where(row == 2, lo, jnp.where(row < 6, 1.0, 0.0))))
    chunk = jnp.concatenate([wide, aux, prb[...].astype(F32)], axis=0)
    own[0:ROWS, :] = chunk[:, :128].astype(BF)
    tail = chunk[:, 128:]
    own[ROWS:FOLD, :] = jnp.concatenate([tail[:ROWS // 2], tail[ROWS // 2:]], axis=1).astype(BF)
    rbuf[0, core] = own[...]

    pl.semaphore_wait(barrier, 1 + 15 * 4)

    def share():
        return pltpu.make_async_remote_copy(
            src_ref=own, dst_ref=rbuf.at[0, core], send_sem=hsend, recv_sem=hrecv,
            device_id=sibling, device_id_type=MESH)

    def row_copy(j):
        return pltpu.make_async_remote_copy(
            src_ref=own, dst_ref=rbuf.at[2 * j, core], send_sem=rsend.at[j], recv_sem=rrecv.at[j // 2, core],
            device_id=device(xh, z, (place - 2 * j + PLACES) % PLACES, j % 2), device_id_type=MESH)

    def across(j):
        slot = jnp.where(xl == 1, 2 * j + 1, (2 * j + 15) % PLACES)
        return pltpu.make_async_remote_copy(
            src_ref=rbuf.at[2 * j], dst_ref=rbuf.at[slot], send_sem=xsend.at[j // 2], recv_sem=xrecv.at[slot // 4],
            device_id=device(xh, z, place + 1 - 2 * xl, core), device_id_type=MESH)

    def around():
        return pltpu.make_async_remote_copy(
            src_ref=rbuf.at[12], dst_ref=rbuf.at[8], send_sem=asend, recv_sem=arecv,
            device_id=device(xh, z, (place + 4) % PLACES, 0), device_id_type=MESH)

    def forward(slot):
        return pltpu.make_async_remote_copy(
            src_ref=rbuf.at[slot], dst_ref=rbuf.at[slot], send_sem=fsend.at[slot % 2 * 4 + slot // 4], recv_sem=frecv.at[slot % 2 * 4 + slot // 4],
            device_id=sibling, device_id_type=MESH)

    def column_copy(taker, h):
        dx, dz = STEPS[taker][h]
        return pltpu.make_async_remote_copy(
            src_ref=own, dst_ref=cbuf.at[h, core], send_sem=csend.at[taker, h], recv_sem=crecv.at[h, core],
            device_id=device((xh - dx + 2) % 2, (z - dz + 8) % 8, place, taker), device_id_type=MESH)

    def relay(taker, h):
        return pltpu.make_async_remote_copy(
            src_ref=cbuf.at[3], dst_ref=cbuf.at[h], send_sem=csend.at[taker, h], recv_sem=lrecv.at[h // 2],
            device_id=device(xh, (z - STEPS[taker][h][1] + 8) % 8, place, taker), device_id_type=MESH)

    def last_relay():
        return pltpu.make_async_remote_copy(
            src_ref=cbuf.at[1], dst_ref=cbuf.at[4], send_sem=lsend, recv_sem=lrecv.at[2],
            device_id=device(xh, (z + jnp.where(core == 0, 2, 6)) % 8, place, other), device_id_type=MESH)

    def trade(pair):
        return pltpu.make_async_remote_copy(
            src_ref=yr.at[pl.ds((2 * pair + other) * 3, 3)], dst_ref=pbuf.at[pair], send_sem=psend.at[pair], recv_sem=precv.at[pair],
            device_id=sibling, device_id_type=MESH)

    def row_sum(pos, c):
        return pltpu.make_async_remote_copy(
            src_ref=yr.at[pl.ds(pos * 3 + c, 2)], dst_ref=ybuf.at[pos],
            send_sem=ysend.at[pos // 2, c], recv_sem=yrecv.at[pos],
            device_id=device(xh, z, (place + chip_step(pos)) % PLACES, c), device_id_type=MESH)

    def column_sum(h, c):
        dx, dz = chosen(h)
        return pltpu.make_async_remote_copy(
            src_ref=yc.at[h, pl.ds(c, 2)], dst_ref=zbuf.at[core, h],
            send_sem=zsend.at[h, c], recv_sem=zrecv.at[core, h],
            device_id=device((xh + dx) % 2, (z + dz) % 8, place, c), device_id_type=MESH)

    def arrived(dst, sem):
        pltpu.make_async_remote_copy(
            src_ref=dst, dst_ref=dst, send_sem=fsend.at[0], recv_sem=sem, device_id=sibling, device_id_type=MESH).wait_recv()

    share().start()
    row_copy(1).start()
    column_copy(1, 3).start()
    column_copy(0, 0).start()
    row_copy(2).start()
    column_copy(1, 0).start()
    row_copy(3).start()
    row_copy(6).start()
    column_copy(0, 1).start()
    for j in (7, 5):
        row_copy(j).start()

    def pass_even(j):
        @pl.when(core == j % 2)
        def _():
            if j == 4:
                arrived(rbuf.at[8], arecv)
            else:
                for half in range(2):
                    arrived(rbuf.at[2 * j, half], rrecv.at[j // 2, half])
            if j == 6:
                around().start()
            forward(2 * j).start()
            across(j).start()

    def pass_odd(j):
        @pl.when(core == (j + xl) % 2)
        def _():
            arrived(rbuf.at[2 * j + 1], xrecv.at[j // 2])
            forward(2 * j + 1).start()

    def collect(pair):
        for t in range(2):
            slot = chip_step(2 * pair + t)
            j, odd = slot // 2, slot % 2

            @pl.when(jnp.logical_and(slot > 0, core != (j + odd * xl) % 2))
            def _():
                arrived(rbuf.at[slot], frecv.at[slot % 2 * 4 + slot // 4])
        prepare(pair)

    def prepare(pair):
        six = tiles_of(rbuf[chip_step(2 * pair)]) + tiles_of(rbuf[chip_step(2 * pair + 1)])
        for b in range(3):
            block = jnp.concatenate([six[2 * b], six[2 * b + 1]], axis=1)
            lb = 3 * pair + b
            feat = block[:FEAT].astype(BF)
            for piece in range(3):
                rw[lb, piece * FEAT:(piece + 1) * FEAT, :] = feat
            rw[lb, 3 * FEAT:, :] = block[FEAT:FEAT + AUX].astype(BF)
            probes = block[FEAT + AUX:]
            left, right = weights(FULL, lb)
            lane = lax.broadcasted_iota(jnp.int32, (PROBES, LANES), 1)
            rv[0, lb] = probes.astype(BF)
            rv[1, lb] = (probes * jnp.where(lane < 128, left, right)).astype(BF)

    def column(h):
        both = jnp.concatenate(tiles_of(cbuf[h]), axis=1)
        scaled = both[:FEAT] * (-10.0 / 3.0)
        hi = scaled.astype(BF).astype(F32)
        mid = (scaled - hi).astype(BF).astype(F32)
        aux = both[FEAT:FEAT + AUX]
        row = lax.broadcasted_iota(jnp.int32, (AUX, CHIP), 0)
        swapped = jnp.where(row < 3, 1.0, jnp.where(row < 6, pltpu.roll(aux, 3, 0), 0.0))
        cpm[h] = jnp.concatenate([hi, mid, scaled - hi - mid, swapped], axis=0).T.astype(BF)
        cv[h] = both[FEAT + AUX:].astype(BF)

    def halves(h):
        for half in range(2):
            arrived(cbuf.at[h, half], crecv.at[h, half])

    def cross(step, b):
        h, lb = tile_of(step, b)
        m[b] = jnp.maximum(jnp.dot(cpm[h], rw[lb], preferred_element_type=F32), 1e-30)

    def entries(b):
        d = m[b]
        t = d * lax.rsqrt(d)
        e = jnp.exp2(t * (-math.sqrt(3.0) * math.log2(math.e)))
        p = t + math.sqrt(0.75)
        return ((p * p + 0.25) * e).astype(BF)

    def products(step, b, kern):
        h, lb = tile_of(step, b)
        mine = jnp.where(h >= FULL, 1, 0)
        left, right = weights(h, lb)
        part = jnp.dot(cv[h], kern, preferred_element_type=F32)
        yr[2 * lb] += part[:, :128] * left
        yr[2 * lb + 1] += part[:, 128:] * right
        part = lax.dot_general(rv[mine, lb], kern, (((1,), (1,)), ((), ())), preferred_element_type=F32)
        for tile in range(3):
            yc[h, tile] += part[:, tile * 128:(tile + 1) * 128]

    def send_rows(pair):
        slot = 2 * pair + core
        arrived(pbuf.at[pair], precv.at[pair])
        at = pl.ds(slot * 3, 3)
        yr[at] = yr[at] + pbuf[pair]

        @pl.when(slot > 0)
        def _():
            row_sum(slot, 0).start()
        row_sum(slot, 1).start()

    def send_columns(h):
        for c in range(2):
            if STEPS[0][h] == (0, 0):
                @pl.when(jnp.logical_or(core == 1, c == 1))
                def _():
                    column_sum(h, c).start()
            else:
                column_sum(h, c).start()

    arrived(rbuf.at[0, other], hrecv)

    @pl.when(core == 0)
    def _():
        across(0).start()
        cbuf[3] = rbuf[0]

    pass_even(1)

    @pl.when(core == 1)
    def _():
        halves(3)
        for taker, h in RELAYED:
            relay(taker, h).start()

    column(3)
    collect(0)
    halves(0)
    column(0)
    pass_even(2)
    for b in range(COLS):
        cross(0, b)

    def tiles(step):
        before, after = jnp.maximum(step - 1, 0), jnp.minimum(step + 1, WORK - 1)
        for b in range(COLS):
            kern = entries(b)
            cross(after, b)
            products(before, b, k[b])
            k[b] = kern

    def arrivals(count, events):
        for when, evens, odds, pairs in events:
            @pl.when(count == when)
            def _():
                for j in evens:
                    pass_even(j)
                for j in odds:
                    pass_odd(j)
                for pair in pairs:
                    collect(pair)

    def work(step, _):
        arrivals(step, ((0, (6,), (0,), (1,)), (1, (3,), (1,), (2,))))
        tiles(step)
        return 0

    def work_two(half, _):
        @pl.when(half < 5)
        def _():
            arrivals(half, ((1, (7, 5), (), ()), (2, (4,), (2,), ()), (3, (), (), (3,)), (4, (), (3, 4, 5, 6, 7), ())))

            @pl.when(half == 1)
            def _():
                @pl.when(core == 0)
                def _():
                    halves(1)

                @pl.when(core == 1)
                def _():
                    arrived(cbuf.at[1], lrecv.at[0])
                last_relay().start()
                arrived(cbuf.at[2], lrecv.at[1])

                def middle(h, _):
                    column(h)
                    return 0
                lax.fori_loop(1, 3, middle, 0)

            @pl.when(half == 3)
            def _():
                arrived(cbuf.at[4], lrecv.at[2])
                column(4)

        @pl.when(half >= 5)
        def _():
            arrivals(half, ((5, (), (), (4,)), (6, (), (), (5,)), (7, (), (), (6,)), (8, (), (), (7,))))

        tiles(2 * half)
        tiles(2 * half + 1)

        @pl.when(half >= 5)
        def _():
            for when, trades, sends, chunks in ((5, (3, 0), (), ()), (6, (1, 2), (3, 0), ()), (7, (4,), (1, 2), (3, 4)),
                                                (8, (5,), (4,), ()), (9, (6,), (5,), ())):
                @pl.when(half == when)
                def _():
                    for pair in trades:
                        trade(pair).start()
                    for pair in sends:
                        send_rows(pair)
                    for h in chunks:
                        send_columns(h)
        return 0

    lax.fori_loop(0, 2, work, 0)
    lax.fori_loop(1, WORK // 2, work_two, 0)
    for b in range(COLS):
        products(WORK - 1, b, k[b])
    trade(7).start()
    send_rows(6)
    for h in (2, 1, 0):
        send_columns(h)
    send_rows(7)

    share().wait_send()
    last_relay().wait_send()
    for taker, h in DIRECT:
        column_copy(taker, h).wait_send()

    @pl.when(core == 1)
    def _():
        for taker, h in RELAYED:
            relay(taker, h).wait_send()

    @pl.when(core == 0)
    def _():
        across(0).wait_send()
        around().wait_send()

    @pl.loop(1, PLACES // 2)
    def _(j):
        @pl.when(j != 4)
        def _():
            row_copy(j).wait_send()

        @pl.when(core == j % 2)
        def _():
            forward(2 * j).wait_send()
            across(j).wait_send()

    @pl.loop(0, PLACES // 2)
    def _(j):
        @pl.when(core == (j + xl) % 2)
        def _():
            forward(2 * j + 1).wait_send()

    @pl.loop(0, PLACES // 2)
    def _(j):
        trade(j).wait_send()

        @pl.when(2 * j + core > 0)
        def _():
            row_sum(2 * j + core, 0).wait_send()
        row_sum(2 * j + core, 1).wait_send()

    for h in range(COLS):
        for c in range(2):
            if STEPS[0][h] == (0, 0):
                @pl.when(jnp.logical_or(core == 1, c == 1))
                def _():
                    column_sum(h, c).wait_send()
            else:
                column_sum(h, c).wait_send()

    @pl.when(core == 0)
    def _():
        ybuf[0] = yr[0:2]
        zbuf[0, 3] = yc[3, 0:2]

    @pl.when(core == 1)
    def _():
        arrived(ybuf.at[0], yrecv.at[0])
        arrived(zbuf.at[0, 3], zrecv.at[0, 3])

    def add_rows(slot, total):
        arrived(ybuf.at[slot], yrecv.at[slot])
        return total + ybuf[slot]

    total = lax.fori_loop(1, PLACES, add_rows, ybuf[0] + zbuf[0, 3])
    for h in (3, 4, 2, 1, 0):
        for taker in range(2):
            if STEPS[taker][h] != (0, 0):
                arrived(zbuf.at[taker, h], zrecv.at[taker, h])
                total = total + zbuf[taker, h]
    total = total * scale
    main = jnp.where(core == 0, total[0], total[1])
    tail = jnp.where(core == 0, total[1], pltpu.roll(total[0], 64, 1))
    out[:, 0:128] = main
    out[:, 128:OWN] = tail[:, 0:64]


def on_device(points, probes):
    total = points.shape[1] * lax.axis_size("loop") * lax.axis_size("grp")
    vmem, dma = pltpu.VMEM, pltpu.SemaphoreType.DMA
    return pl.pallas_call(
        lambda *refs: kernel(float(total) ** (-0.5), *refs),
        out_shape=jax.ShapeDtypeStruct((PROBES, OWN), F32),
        in_specs=[pl.BlockSpec(memory_space=pltpu.HBM)] * 2,
        out_specs=pl.BlockSpec(memory_space=vmem),
        scratch_shapes=[
            vmem((FEAT, OWN), BF),
            vmem((PROBES, OWN), BF),
            vmem((FOLD, 128), BF),
            vmem((PLACES, 2, FOLD, 128), BF),
            vmem((COLS, 2, FOLD, 128), BF),
            vmem((COLS, CHIP, DEPTH), BF),
            vmem((COLS, PROBES, CHIP), BF),
            vmem((BLOCKS, DEPTH, LANES), BF),
            vmem((2, BLOCKS, PROBES, LANES), BF),
            vmem((PLACES * 3, PROBES, 128), F32),
            vmem((COLS, 3, PROBES, 128), F32),
            vmem((PLACES // 2, 3, PROBES, 128), F32),
            vmem((PLACES, 2, PROBES, 128), F32),
            vmem((2, COLS, 2, PROBES, 128), F32),
            vmem((COLS, CHIP, LANES), F32),
            vmem((COLS, CHIP, LANES), BF),
            dma, dma, dma, dma, dma((PLACES // 2,)), dma((PLACES // 4, 2)), dma((PLACES // 4,)), dma((PLACES // 4,)),
            dma((PLACES // 2,)), dma((PLACES // 2,)), dma((2, COLS)), dma((COLS, 2)), dma, dma((3,)),
            dma((PLACES // 2,)), dma((PLACES // 2,)), dma((PLACES // 2, 2)), dma((PLACES,)), dma((COLS, 2)), dma((2, COLS)), dma((2,)),
        ],
        compiler_params=pltpu.CompilerParams(
            collective_id=0, has_side_effects=True, vmem_limit_bytes=40 * 1024 * 1024
        ),
        name="matern_product",
    )(points, probes)


def solution(mesh):
    specs = P(None, ("loop", "grp"))
    return jax.shard_map(on_device, mesh=mesh, in_specs=(specs, specs), out_specs=specs, check_vma=False)
```

```python
import math

import jax
import jax.numpy as jnp
from jax import lax
from jax.experimental import pallas as pl
from jax.experimental.pallas import tpu as pltpu
from jax.sharding import PartitionSpec as P

MESH = pl.DeviceIdType.MESH
BF = jnp.bfloat16
F32 = jnp.float32
FEAT, PROBES, OWN = 64, 16, 192
AUX = 16
ROWS = FEAT + AUX + PROBES
FOLD = ROWS + ROWS // 2
DEPTH = 3 * FEAT + AUX
PLACES = 16
CHIP = 2 * OWN
LANES = 256
BLOCKS = PLACES * CHIP // LANES
STEPS = (((0, 1), (0, 6), (1, 7), (0, 0), (1, 4)),
         ((0, 3), (1, 2), (1, 5), (1, 0), (0, 4)))
FULL, COLS = 3, 5
DIRECT = ((1, 3), (0, 0), (1, 0), (0, 1))
RELAYED = ((1, 1), (0, 2), (1, 2))
NEAR, NEXT = 9, 12
BOTH = 14
WORK = (BOTH * COLS + (BLOCKS - BOTH) * FULL) // COLS


def device(xh, z, place, core):
    return ((z // 4 * 4 + xh * 2 + place % 2) * 2 + core, place // 2 * 4 + z % 4)


def tile_of(step, b):
    flat = step * COLS + b
    two, three = flat - 2 * NEAR, flat - 4 * NEAR
    four = three - COLS * (NEXT - NEAR)
    five = four - NEAR
    rest = five - COLS * (BOTH - NEXT)
    turn = jnp.where(four < 0, three, five) % 5
    turn = jnp.where(turn == 1, 3, jnp.where(jnp.logical_or(turn == 2, turn == 3), turn - 1, turn))
    h = jnp.where(rest < 0, turn, rest % 3)
    h = jnp.where(jnp.logical_and(four >= 0, five < 0), 4, jnp.where(three < 0, two % 2 + 1, h))
    lb = jnp.where(rest < 0, NEXT + five // 5, BOTH + rest // 3)
    lb = jnp.where(four < 0, NEAR + three // 5, jnp.where(five < 0, four, lb))
    lb = jnp.where(three < 0, two // 2, lb)
    return jnp.where(two < 0, flat % 2 * 3, h), jnp.where(two < 0, flat // 2, lb)


def chip_step(pos):
    step = jnp.where(pos < 3, 2 * pos, jnp.where(pos < 10, 2 * pos - 5, pos - 1))
    step = jnp.where(pos == 4, 6, jnp.where(pos == 5, 3, jnp.where(pos == 6, 5, step)))
    step = jnp.where(pos == 7, 8, jnp.where(pos == 8, 7, jnp.where(pos == 9, 14, step)))
    return jnp.where(pos == 15, 15, step)


def weights(h, lb):
    mine = h >= FULL
    left = jnp.where(jnp.logical_and(mine, among(lb, (0, 1, 11))), 0.5, 1.0)
    right = jnp.where(jnp.logical_and(mine, among(lb, (0, 10, 11))), 0.5, 1.0)
    right = jnp.where(jnp.logical_and(mine, lb == 13), 0.0, right)
    return left, right


def among(value, options):
    hit = value == options[0]
    for option in options[1:]:
        hit = jnp.logical_or(hit, value == option)
    return hit


def tiles_of(halves):
    first, second = halves[0].astype(F32), halves[1].astype(F32)
    low = lax.broadcasted_iota(jnp.int32, (ROWS // 2, 128), 1) < 64
    f0, f1 = first[ROWS:], second[ROWS:]
    top = jnp.where(low, f0, pltpu.roll(f1, 64, 1))
    bottom = jnp.where(low, pltpu.roll(f0, 64, 1), f1)
    return first[:ROWS], jnp.concatenate([top, bottom], axis=0), second[:ROWS]


def kernel(scale, points, probes, out, pts, prb, own, rbuf, cbuf, cpm, cv, rw, rv, yr, yc, pbuf, ybuf, zbuf, m, k,
           hsend, hrecv, asend, arecv, rsend, rrecv, xsend, xrecv, fsend, frecv, csend, crecv, lsend, lrecv, psend, precv, ysend, yrecv,
           zsend, zrecv, isem):
    loop, grp = lax.axis_index("loop"), lax.axis_index("grp")
    core, x, z = loop % 2, (loop // 2) % 4, loop // 8 * 4 + grp % 4
    other = 1 - core
    xh, xl, place = x // 2, x % 2, grp // 4 * 2 + x % 2
    sibling = device(xh, z, place, other)

    def chosen(h):
        (ax, az), (bx, bz) = STEPS[0][h], STEPS[1][h]
        return jnp.where(core == 0, ax, bx), jnp.where(core == 0, az, bz)

    barrier = pltpu.get_barrier_semaphore()
    pl.semaphore_signal(barrier, inc=1, device_id=sibling, device_id_type=MESH)

    @pl.loop(1, 16)
    def _(step):
        for c in range(2):
            pl.semaphore_signal(barrier, inc=1, device_id=device((xh + step // 8) % 2, (z + step) % 8, place, c), device_id_type=MESH)

    @pl.loop(1, 16)
    def _(step):
        for c in range(2):
            pl.semaphore_signal(barrier, inc=1, device_id=device(xh, z, (place + step) % PLACES, c), device_id_type=MESH)

    copies = [pltpu.make_async_copy(points, pts, isem.at[0]), pltpu.make_async_copy(probes, prb, isem.at[1])]
    for copy in copies:
        copy.start()
    yr[...] = jnp.zeros_like(yr)
    yc[...] = jnp.zeros_like(yc)
    k[...] = jnp.zeros_like(k)
    for copy in copies:
        copy.wait()

    wide = pts[...].astype(F32)
    n = jnp.sum(wide * wide, axis=0, keepdims=True) * (5.0 / 3.0)
    hi = n.astype(BF).astype(F32)
    mid = (n - hi).astype(BF).astype(F32)
    lo = n - hi - mid
    row = lax.broadcasted_iota(jnp.int32, (AUX, OWN), 0)
    aux = jnp.where(row == 0, hi, jnp.where(row == 1, mid, jnp.where(row == 2, lo, jnp.where(row < 6, 1.0, 0.0))))
    chunk = jnp.concatenate([wide, aux, prb[...].astype(F32)], axis=0)
    own[0:ROWS, :] = chunk[:, :128].astype(BF)
    tail = chunk[:, 128:]
    own[ROWS:FOLD, :] = jnp.concatenate([tail[:ROWS // 2], tail[ROWS // 2:]], axis=1).astype(BF)
    rbuf[0, core] = own[...]

    pl.semaphore_wait(barrier, 1 + 15 * 4)

    def share():
        return pltpu.make_async_remote_copy(
            src_ref=own, dst_ref=rbuf.at[0, core], send_sem=hsend, recv_sem=hrecv,
            device_id=sibling, device_id_type=MESH)

    def row_copy(j):
        return pltpu.make_async_remote_copy(
            src_ref=own, dst_ref=rbuf.at[2 * j, core], send_sem=rsend.at[j], recv_sem=rrecv.at[j // 2, core],
            device_id=device(xh, z, (place - 2 * j + PLACES) % PLACES, j % 2), device_id_type=MESH)

    def across(j):
        slot = jnp.where(xl == 1, 2 * j + 1, (2 * j + 15) % PLACES)
        return pltpu.make_async_remote_copy(
            src_ref=rbuf.at[2 * j], dst_ref=rbuf.at[slot], send_sem=xsend.at[j // 2], recv_sem=xrecv.at[slot // 4],
            device_id=device(xh, z, place + 1 - 2 * xl, core), device_id_type=MESH)

    def around():
        return pltpu.make_async_remote_copy(
            src_ref=rbuf.at[12], dst_ref=rbuf.at[8], send_sem=asend, recv_sem=arecv,
            device_id=device(xh, z, (place + 4) % PLACES, 0), device_id_type=MESH)

    def forward(slot):
        return pltpu.make_async_remote_copy(
            src_ref=rbuf.at[slot], dst_ref=rbuf.at[slot], send_sem=fsend.at[slot % 2 * 4 + slot // 4], recv_sem=frecv.at[slot % 2 * 4 + slot // 4],
            device_id=sibling, device_id_type=MESH)

    def column_copy(taker, h):
        dx, dz = STEPS[taker][h]
        return pltpu.make_async_remote_copy(
            src_ref=own, dst_ref=cbuf.at[h, core], send_sem=csend.at[taker, h], recv_sem=crecv.at[h, core],
            device_id=device((xh - dx + 2) % 2, (z - dz + 8) % 8, place, taker), device_id_type=MESH)

    def relay(taker, h):
        return pltpu.make_async_remote_copy(
            src_ref=cbuf.at[3], dst_ref=cbuf.at[h], send_sem=csend.at[taker, h], recv_sem=lrecv.at[h // 2],
            device_id=device(xh, (z - STEPS[taker][h][1] + 8) % 8, place, taker), device_id_type=MESH)

    def last_relay():
        return pltpu.make_async_remote_copy(
            src_ref=cbuf.at[1], dst_ref=cbuf.at[4], send_sem=lsend, recv_sem=lrecv.at[2],
            device_id=device(xh, (z + jnp.where(core == 0, 2, 6)) % 8, place, other), device_id_type=MESH)

    def trade(pair):
        return pltpu.make_async_remote_copy(
            src_ref=yr.at[pl.ds((2 * pair + other) * 3, 3)], dst_ref=pbuf.at[pair], send_sem=psend.at[pair], recv_sem=precv.at[pair],
            device_id=sibling, device_id_type=MESH)

    def row_sum(pos, c):
        return pltpu.make_async_remote_copy(
            src_ref=yr.at[pl.ds(pos * 3 + c, 2)], dst_ref=ybuf.at[pos],
            send_sem=ysend.at[pos // 2, c], recv_sem=yrecv.at[pos],
            device_id=device(xh, z, (place + chip_step(pos)) % PLACES, c), device_id_type=MESH)

    def column_sum(h, c):
        dx, dz = chosen(h)
        return pltpu.make_async_remote_copy(
            src_ref=yc.at[h, pl.ds(c, 2)], dst_ref=zbuf.at[core, h],
            send_sem=zsend.at[h, c], recv_sem=zrecv.at[core, h],
            device_id=device((xh + dx) % 2, (z + dz) % 8, place, c), device_id_type=MESH)

    def arrived(dst, sem):
        pltpu.make_async_remote_copy(
            src_ref=dst, dst_ref=dst, send_sem=fsend.at[0], recv_sem=sem, device_id=sibling, device_id_type=MESH).wait_recv()

    share().start()
    row_copy(1).start()
    column_copy(1, 3).start()
    column_copy(0, 0).start()
    row_copy(2).start()
    column_copy(1, 0).start()
    row_copy(3).start()
    row_copy(6).start()
    column_copy(0, 1).start()
    for j in (7, 5):
        row_copy(j).start()

    def pass_even(j):
        @pl.when(core == j % 2)
        def _():
            if j == 4:
                arrived(rbuf.at[8], arecv)
            else:
                for half in range(2):
                    arrived(rbuf.at[2 * j, half], rrecv.at[j // 2, half])
            if j == 6:
                around().start()
            forward(2 * j).start()
            across(j).start()

    def pass_odd(j):
        @pl.when(core == (j + xl) % 2)
        def _():
            arrived(rbuf.at[2 * j + 1], xrecv.at[j // 2])
            forward(2 * j + 1).start()

    def collect(pair):
        for t in range(2):
            slot = chip_step(2 * pair + t)
            j, odd = slot // 2, slot % 2

            @pl.when(jnp.logical_and(slot > 0, core != (j + odd * xl) % 2))
            def _():
                arrived(rbuf.at[slot], frecv.at[slot % 2 * 4 + slot // 4])
        prepare(pair)

    def prepare(pair):
        six = tiles_of(rbuf[chip_step(2 * pair)]) + tiles_of(rbuf[chip_step(2 * pair + 1)])
        for b in range(3):
            block = jnp.concatenate([six[2 * b], six[2 * b + 1]], axis=1)
            lb = 3 * pair + b
            feat = block[:FEAT].astype(BF)
            for piece in range(3):
                rw[lb, piece * FEAT:(piece + 1) * FEAT, :] = feat
            rw[lb, 3 * FEAT:, :] = block[FEAT:FEAT + AUX].astype(BF)
            probes = block[FEAT + AUX:]
            left, right = weights(FULL, lb)
            lane = lax.broadcasted_iota(jnp.int32, (PROBES, LANES), 1)
            rv[0, lb] = probes.astype(BF)
            rv[1, lb] = (probes * jnp.where(lane < 128, left, right)).astype(BF)

    def column(h):
        both = jnp.concatenate(tiles_of(cbuf[h]), axis=1)
        scaled = both[:FEAT] * (-10.0 / 3.0)
        hi = scaled.astype(BF).astype(F32)
        mid = (scaled - hi).astype(BF).astype(F32)
        aux = both[FEAT:FEAT + AUX]
        row = lax.broadcasted_iota(jnp.int32, (AUX, CHIP), 0)
        swapped = jnp.where(row < 3, 1.0, jnp.where(row < 6, pltpu.roll(aux, 3, 0), 0.0))
        cpm[h] = jnp.concatenate([hi, mid, scaled - hi - mid, swapped], axis=0).T.astype(BF)
        cv[h] = both[FEAT + AUX:].astype(BF)

    def halves(h):
        for half in range(2):
            arrived(cbuf.at[h, half], crecv.at[h, half])

    def cross(step, b):
        h, lb = tile_of(step, b)
        m[b] = jnp.maximum(jnp.dot(cpm[h], rw[lb], preferred_element_type=F32), 1e-30)

    def entries(b):
        d = m[b]
        t = d * lax.rsqrt(d)
        e = jnp.exp2(t * (-math.sqrt(3.0) * math.log2(math.e)))
        p = t + math.sqrt(0.75)
        return ((p * p + 0.25) * e).astype(BF)

    def products(step, b, kern):
        h, lb = tile_of(step, b)
        mine = jnp.where(h >= FULL, 1, 0)
        left, right = weights(h, lb)
        part = jnp.dot(cv[h], kern, preferred_element_type=F32)
        yr[2 * lb] += part[:, :128] * left
        yr[2 * lb + 1] += part[:, 128:] * right
        part = lax.dot_general(rv[mine, lb], kern, (((1,), (1,)), ((), ())), preferred_element_type=F32)
        for tile in range(3):
            yc[h, tile] += part[:, tile * 128:(tile + 1) * 128]

    def send_rows(pair):
        slot = 2 * pair + core
        arrived(pbuf.at[pair], precv.at[pair])
        at = pl.ds(slot * 3, 3)
        yr[at] = yr[at] + pbuf[pair]

        @pl.when(slot > 0)
        def _():
            row_sum(slot, 0).start()
        row_sum(slot, 1).start()

    def send_columns(h):
        for c in range(2):
            if STEPS[0][h] == (0, 0):
                @pl.when(jnp.logical_or(core == 1, c == 1))
                def _():
                    column_sum(h, c).start()
            else:
                column_sum(h, c).start()

    arrived(rbuf.at[0, other], hrecv)

    @pl.when(core == 0)
    def _():
        across(0).start()
        cbuf[3] = rbuf[0]

    pass_even(1)

    @pl.when(core == 1)
    def _():
        halves(3)
        for taker, h in RELAYED:
            relay(taker, h).start()

    column(3)
    collect(0)
    halves(0)
    column(0)
    pass_even(2)
    for b in range(COLS):
        cross(0, b)

    def tiles(step):
        before, after = jnp.maximum(step - 1, 0), jnp.minimum(step + 1, WORK - 1)
        for b in range(COLS):
            kern = entries(b)
            cross(after, b)
            products(before, b, k[b])
            k[b] = kern

    def arrivals(count, events):
        for when, evens, odds, pairs in events:
            @pl.when(count == when)
            def _():
                for j in evens:
                    pass_even(j)
                for j in odds:
                    pass_odd(j)
                for pair in pairs:
                    collect(pair)

    def work(step, _):
        arrivals(step, ((0, (6,), (0,), (1,)), (1, (3,), (1,), (2,))))
        tiles(step)
        return 0

    def work_two(half, _):
        @pl.when(half < 5)
        def _():
            arrivals(half, ((1, (7, 5), (), ()), (2, (4,), (2,), ()), (3, (), (), (3,)), (4, (), (3, 4, 5, 6, 7), ())))

            @pl.when(half == 1)
            def _():
                @pl.when(core == 0)
                def _():
                    halves(1)

                @pl.when(core == 1)
                def _():
                    arrived(cbuf.at[1], lrecv.at[0])
                last_relay().start()
                arrived(cbuf.at[2], lrecv.at[1])

                def middle(h, _):
                    column(h)
                    return 0
                lax.fori_loop(1, 3, middle, 0)

            @pl.when(half == 3)
            def _():
                arrived(cbuf.at[4], lrecv.at[2])
                column(4)

        @pl.when(half >= 5)
        def _():
            arrivals(half, ((5, (), (), (4,)), (6, (), (), (5,)), (7, (), (), (6,)), (8, (), (), (7,))))

        tiles(2 * half)
        tiles(2 * half + 1)

        @pl.when(half >= 5)
        def _():
            for when, trades, sends, chunks in ((5, (3, 0), (), ()), (6, (1, 2), (3, 0), ()), (7, (4,), (1, 2), (3, 4)),
                                                (8, (5,), (4,), ()), (9, (6,), (5,), ())):
                @pl.when(half == when)
                def _():
                    for pair in trades:
                        trade(pair).start()
                    for pair in sends:
                        send_rows(pair)
                    for h in chunks:
                        send_columns(h)
        return 0

    lax.fori_loop(0, 2, work, 0)
    lax.fori_loop(1, WORK // 2, work_two, 0)
    for b in range(COLS):
        products(WORK - 1, b, k[b])
    trade(7).start()
    send_rows(6)
    for h in (2, 1, 0):
        send_columns(h)
    send_rows(7)

    share().wait_send()
    last_relay().wait_send()
    for taker, h in DIRECT:
        column_copy(taker, h).wait_send()

    @pl.when(core == 1)
    def _():
        for taker, h in RELAYED:
            relay(taker, h).wait_send()

    @pl.when(core == 0)
    def _():
        across(0).wait_send()
        around().wait_send()

    @pl.loop(1, PLACES // 2)
    def _(j):
        @pl.when(j != 4)
        def _():
            row_copy(j).wait_send()

        @pl.when(core == j % 2)
        def _():
            forward(2 * j).wait_send()
            across(j).wait_send()

    @pl.loop(0, PLACES // 2)
    def _(j):
        @pl.when(core == (j + xl) % 2)
        def _():
            forward(2 * j + 1).wait_send()

    @pl.loop(0, PLACES // 2)
    def _(j):
        trade(j).wait_send()

        @pl.when(2 * j + core > 0)
        def _():
            row_sum(2 * j + core, 0).wait_send()
        row_sum(2 * j + core, 1).wait_send()

    for h in range(COLS):
        for c in range(2):
            if STEPS[0][h] == (0, 0):
                @pl.when(jnp.logical_or(core == 1, c == 1))
                def _():
                    column_sum(h, c).wait_send()
            else:
                column_sum(h, c).wait_send()

    @pl.when(core == 0)
    def _():
        ybuf[0] = yr[0:2]
        zbuf[0, 3] = yc[3, 0:2]

    @pl.when(core == 1)
    def _():
        arrived(ybuf.at[0], yrecv.at[0])
        arrived(zbuf.at[0, 3], zrecv.at[0, 3])

    def add_rows(slot, total):
        arrived(ybuf.at[slot], yrecv.at[slot])
        return total + ybuf[slot]

    total = lax.fori_loop(1, PLACES, add_rows, ybuf[0] + zbuf[0, 3])
    for h in (3, 4, 2, 1, 0):
        for taker in range(2):
            if STEPS[taker][h] != (0, 0):
                arrived(zbuf.at[taker, h], zrecv.at[taker, h])
                total = total + zbuf[taker, h]
    total = total * scale
    main = jnp.where(core == 0, total[0], total[1])
    tail = jnp.where(core == 0, total[1], pltpu.roll(total[0], 64, 1))
    out[:, 0:128] = main
    out[:, 128:OWN] = tail[:, 0:64]


def on_device(points, probes):
    total = points.shape[1] * lax.axis_size("loop") * lax.axis_size("grp")
    vmem, dma = pltpu.VMEM, pltpu.SemaphoreType.DMA
    return pl.pallas_call(
        lambda *refs: kernel(float(total) ** (-0.5), *refs),
        out_shape=jax.ShapeDtypeStruct((PROBES, OWN), F32),
        in_specs=[pl.BlockSpec(memory_space=pltpu.HBM)] * 2,
        out_specs=pl.BlockSpec(memory_space=vmem),
        scratch_shapes=[
            vmem((FEAT, OWN), BF),
            vmem((PROBES, OWN), BF),
            vmem((FOLD, 128), BF),
            vmem((PLACES, 2, FOLD, 128), BF),
            vmem((COLS, 2, FOLD, 128), BF),
            vmem((COLS, CHIP, DEPTH), BF),
            vmem((COLS, PROBES, CHIP), BF),
            vmem((BLOCKS, DEPTH, LANES), BF),
            vmem((2, BLOCKS, PROBES, LANES), BF),
            vmem((PLACES * 3, PROBES, 128), F32),
            vmem((COLS, 3, PROBES, 128), F32),
            vmem((PLACES // 2, 3, PROBES, 128), F32),
            vmem((PLACES, 2, PROBES, 128), F32),
            vmem((2, COLS, 2, PROBES, 128), F32),
            vmem((COLS, CHIP, LANES), F32),
            vmem((COLS, CHIP, LANES), BF),
            dma, dma, dma, dma, dma((PLACES // 2,)), dma((PLACES // 4, 2)), dma((PLACES // 4,)), dma((PLACES // 4,)),
            dma((PLACES // 2,)), dma((PLACES // 2,)), dma((2, COLS)), dma((COLS, 2)), dma, dma((3,)),
            dma((PLACES // 2,)), dma((PLACES // 2,)), dma((PLACES // 2, 2)), dma((PLACES,)), dma((COLS, 2)), dma((2, COLS)), dma((2,)),
        ],
        compiler_params=pltpu.CompilerParams(
            collective_id=0, has_side_effects=True, vmem_limit_bytes=60 * 1024 * 1024
        ),
        name="matern_product",
    )(points, probes)


def solution(mesh):
    specs = P(None, ("loop", "grp"))
    return jax.shard_map(on_device, mesh=mesh, in_specs=(specs, specs), out_specs=specs, check_vma=False)
```
